32 devices in a mesh: section: 2 (over core), row: 8 (over z, y), col: 2 (over x).
Axes of the slice: x: 2, y: 2, z: 4, core: 2. Of those that a mesh axis runs over, the one named last changes fastest.
Arguments:
- latents: bfloat16 [8, 4, 256, 1152], P('row', None, 'col'), may hold values from -6 to 6
- timesteps: int32 [8], P('row'), may hold values from 0 to 999
- lengths: int32 [8], P('row'), may hold values from 1 to 1024, 6144 in all
- patch_order: int32 [4], replicated, may hold values from 0 to 3, each once
- ada_weight: bfloat16 [2, 1152, 6, 1152], P('section', 'row', None, 'col'), may hold values from -0.1875 to 0.1875
- qkv_weight: bfloat16 [2, 1152, 3, 1152], P('section', 'row', None, 'col'), may hold values from -1 to 1
- out_weight: bfloat16 [2, 1152, 1152], P('section', 'col', 'row'), may hold values from -0.1875 to 0.1875
- up_weight: bfloat16 [2, 1152, 4608], P('section', 'row', 'col'), may hold values from -0.1875 to 0.1875
- down_weight: bfloat16 [2, 4608, 1152], P('section', 'col', 'row'), may hold values from -0.09375 to 0.09375
- stale_keys: bfloat16 [2, 8, 4, 256, 1152], P('section', 'row', None, None, 'col'), may hold values from -9 to 9
- stale_values: bfloat16 [2, 8, 4, 256, 1152], P('section', 'row', None, None, 'col'), may hold values from -6 to 6
Outputs:
- section_out: bfloat16 [2, 8, 4, 256, 1152], P('section', 'row', None, 'col')
The draws below stay inside these ranges and needn't reach their ends.
Inputs may be any that keep to these rules, and one draw needn't show every extreme that they name: `lengths`: tokens that serve as keys in each request; some request has all 1024. `patch_order`: each of the 4 patches once.
All inputs are finite; a program needn't handle non-finite values. No bound on the sum of `lengths` on one device may be relied on, other than what follows from the above.
Results may differ from the reference program's by a relative error of at most 0.0095.
Values may be sent and summed in bfloat16 or wider, within the bound.
No kernel may reach another device: no remote copies, remote signals or barrier semaphores. Data moves between devices by JAX's collectives and lax.ppermute only.
A program may use at most 128 MiB of HBM per device.

```python
import math
import jax
import jax.numpy as jnp
import numpy as np
from jax import lax

D = 1152
HEADS = 16
HD = 72
FF = 4608
SEQ = 1024
PATCHES = 4
PTOK = 256
SECTIONS = 2
REQUESTS = 8
TSTEPS = 1000
N_COL = 2


def width_signs(key):
    return jax.random.randint(jax.random.fold_in(key, 11), (D,), 0, 2).astype(jnp.float32) * 2.0 - 1.0


def head_signs(key):
    return jax.random.randint(jax.random.fold_in(key, 12), (SECTIONS, HEADS, HD), 0, 2).astype(jnp.float32) * 2.0 - 1.0


def head_strength(key):
    offsets = jax.random.randint(jax.random.fold_in(key, 13), (SECTIONS, 1), 0, HEADS)
    ranks = (jnp.arange(HEADS, dtype=jnp.int32)[None, :] * 5 + offsets) % HEADS
    share = ranks.astype(jnp.float32) / (max(HEADS - 1, 1) * 1.0)
    return 0.5 * jnp.exp(share * math.log(160.0))


def draw_latents(key, part):
    shape = (REQUESTS, PATCHES, PTOK, D)
    noise = jax.random.truncated_normal(jax.random.fold_in(key, 21), -4.0, 4.0, shape, jnp.float32)
    amount = jax.random.uniform(jax.random.fold_in(key, 22), (REQUESTS, PATCHES, PTOK, 1), jnp.float32, 0.4, 1.6)
    return (noise + amount * width_signs(key)).astype(jnp.bfloat16)


def draw_qkv_weight(key, part):
    shape = (SECTIONS, D, 3, D)
    spread = 1.0 / math.sqrt(D)
    noise = jax.random.truncated_normal(jax.random.fold_in(key, 31), -4.0, 4.0, shape, jnp.float32) * spread
    columns = (head_strength(key)[:, :, None] * head_signs(key)).reshape(SECTIONS, 1, D)
    planted = columns * width_signs(key)[None, :, None] / (D * math.sqrt(HD))
    which = (jnp.arange(3, dtype=jnp.int32) == 0).astype(jnp.float32)
    return (noise + planted[:, :, None, :] * which[None, None, :, None]).astype(jnp.bfloat16)


def draw_stale_keys(key, part):
    shape = (SECTIONS, REQUESTS, PATCHES, PTOK, HEADS, HD)
    noise = jax.random.truncated_normal(jax.random.fold_in(key, 41), -5.0, 5.0, shape, jnp.float32)
    share = jax.random.uniform(jax.random.fold_in(key, 42), (SECTIONS, REQUESTS, PATCHES, PTOK, HEADS, 1), jnp.float32, 0.0, 1.0)
    lift = 4.0
    keys = noise + lift * share * head_signs(key)[:, None, None, None, :, :]
    return keys.reshape(SECTIONS, REQUESTS, PATCHES, PTOK, D).astype(jnp.bfloat16)


def touch_ends(values, key, smallest, top_value):
    shape = values.shape
    index_at = [jax.random.randint(jax.random.fold_in(key, axis), (), 0, shape[axis]) for axis in range(len(shape))]
    values = values.at[tuple(index_at)].set(smallest)
    longest = shape.index(max(shape))
    index_at[longest] = (index_at[longest] + 1) % shape[longest]
    return values.at[tuple(index_at)].set(top_value)


def levels(key, shape, cuts, low, top_value):
    level = 1.0
    for dim, blocks in cuts:
        draws = jax.random.uniform(jax.random.fold_in(jax.random.fold_in(key, 6), dim), (blocks,), jnp.float32, low / len(cuts), top_value / len(cuts))
        level = level * jnp.repeat(jnp.exp(draws), shape[dim] // blocks).reshape((-1,) + (1,) * (len(shape) - 1 - dim))
    return level


def split_up(count, total, most, lean):
    loads = [(1 << 20) // math.isqrt(grade ** lean) + 1 for grade in range(2, count + 1)]
    rest, given = total - most - (count - 1), [1] * (count - 1)
    while rest > 0:
        free = [i for i in range(count - 1) if given[i] < most]
        pool, budget = sum([loads[i] for i in free]), rest
        for i in free:
            extra = min(most - given[i], max(1, budget * loads[i] // pool), rest)
            given[i] = given[i] + extra
            rest = rest - extra
    return np.array([most] + given)


def uneven_parts(rng, count, total, reach, lean):
    if count == 2:
        one = jax.random.randint(rng, (), max(1, total - reach), min(reach, total - 1) + 1)
        return jnp.stack([one, total - one])
    sizes = jnp.asarray(split_up(count, total, reach, lean), jnp.int32)
    couples = (count - 1) // 2
    source_of, taker = sizes[1:1 + 2 * couples:2], sizes[2:2 + 2 * couples:2]
    slack = jnp.minimum(source_of - 1, reach - taker)
    passed = jax.random.randint(jax.random.fold_in(rng, 1), (couples,), 0, 1 << 20) % (slack + 1)
    sizes = sizes.at[1:1 + 2 * couples:2].set(source_of - passed).at[2:2 + 2 * couples:2].set(taker + passed)
    return sizes[jax.random.permutation(jax.random.fold_in(rng, 2), count)]


def normal_values(own_key, dims, scale, bound, shards=(), kind=jnp.bfloat16):
    values = scale * jax.random.normal(own_key, dims, jnp.float32)
    if shards:
        values = values * levels(own_key, dims, shards, -0.22, 0.18)
    return jnp.clip(values, -bound, bound).astype(kind)


def setup_inputs(seed: int = 0) -> dict:
    arg_keys = jax.random.split(jax.random.key(seed), 12)
    return {
        "latents": draw_latents(jax.random.fold_in(arg_keys[11], 71), 0),
        "timesteps": touch_ends(jax.random.randint(arg_keys[1], (REQUESTS,), 0, TSTEPS), jax.random.fold_in(arg_keys[1], 1), 0, TSTEPS - 1).astype(jnp.int32),
        "lengths": uneven_parts(arg_keys[2], REQUESTS, REQUESTS * SEQ * 3 // 4, SEQ, 2).astype(jnp.int32),
        "patch_order": jax.random.permutation(arg_keys[3], PATCHES).astype(jnp.int32),
        "ada_weight": normal_values(arg_keys[4], (SECTIONS, D, 6, D), D ** -0.5, 0.1875, ((0, 2), (1, 8), (3, 2))),
        "qkv_weight": draw_qkv_weight(jax.random.fold_in(arg_keys[11], 71), 0),
        "out_weight": normal_values(arg_keys[6], (SECTIONS, D, D), D ** -0.5, 0.1875, ((0, 2), (1, 2), (2, 8))),
        "up_weight": normal_values(arg_keys[7], (SECTIONS, D, FF), D ** -0.5, 0.1875, ((0, 2), (1, 8), (2, 2))),
        "down_weight": normal_values(arg_keys[8], (SECTIONS, FF, D), FF ** -0.5, 0.09375, ((0, 2), (1, 2), (2, 8))),
        "stale_keys": draw_stale_keys(jax.random.fold_in(arg_keys[11], 71), 0),
        "stale_values": normal_values(arg_keys[10], (SECTIONS, REQUESTS, PATCHES, PTOK, D), 1.0, 6.0, ((0, 2), (1, 8), (4, 2))),
    }


def sinusoid(step_ids):
    half_width = D // 2
    frequency = jnp.exp(-math.log(10000.0) * jnp.arange(half_width, dtype=jnp.float32) / half_width)
    angles = step_ids.astype(jnp.float32)[:, None] * frequency[None, :]
    return jnp.concatenate([jnp.cos(angles), jnp.sin(angles)], axis=1)

def layer_norm(inputs):
    center = lax.optimization_barrier(jnp.mean(inputs, axis=-1, keepdims=True))
    spread = lax.optimization_barrier(jnp.mean(jnp.square(inputs - center), axis=-1, keepdims=True))
    return (inputs - center) * lax.rsqrt(spread + 1e-06)

def attend(queries, keys, values, valid_keys):
    scores = jnp.einsum('bqhd,bkhd->bhqk', queries.astype(jnp.float32), keys.astype(jnp.float32)) / math.sqrt(HD)
    scores = jnp.where(valid_keys[:, None, None, :], scores, -1e+30)
    top_score = lax.optimization_barrier(jnp.max(scores, axis=-1, keepdims=True))
    weights = jnp.exp(scores - top_score)
    totals = lax.optimization_barrier(jnp.sum(weights, axis=-1))
    probs = weights.astype(jnp.bfloat16)
    mixed = jnp.einsum('bhqk,bkhd->bqhd', probs.astype(jnp.float32), values.astype(jnp.float32))
    return (mixed / jnp.transpose(totals, (0, 2, 1))[..., None]).astype(jnp.bfloat16)

def grouped_sum(inputs, weight):
    requests, tokens, inner = inputs.shape
    group_width = inner // N_COL
    parts = jnp.einsum('rtgc,gcd->grtd', inputs.reshape(requests, tokens, N_COL, group_width).astype(jnp.float32), weight.reshape(N_COL, group_width, weight.shape[1]).astype(jnp.float32))
    rounded = lax.optimization_barrier(parts.astype(jnp.bfloat16)).astype(jnp.float32)
    return lax.optimization_barrier(jnp.sum(rounded, axis=0))

def run_section(section_in, cond, ada, qkv_w, out_w, up_w, down_w, key_cache, value_cache, valid_keys, patch_order):
    modulation = jnp.einsum('rd,dkc->rkc', cond.astype(jnp.float32), ada.astype(jnp.float32))
    shift_attn = modulation[:, 0][:, None, :]
    scale_attn = modulation[:, 1][:, None, :]
    gate_attn = modulation[:, 2][:, None, :]
    shift_mlp = modulation[:, 3][:, None, :]
    scale_mlp = modulation[:, 4][:, None, :]
    gate_mlp = modulation[:, 5][:, None, :]
    requests = section_in.shape[0]
    results = section_in
    for position in range(PATCHES):
        patch_id = patch_order[position]
        tokens_in = lax.dynamic_index_in_dim(section_in, patch_id, 1, keepdims=False).astype(jnp.float32)
        normed = (layer_norm(tokens_in) * (1.0 + scale_attn) + shift_attn).astype(jnp.bfloat16)
        projected = jnp.einsum('rtd,dkc->rtkc', normed.astype(jnp.float32), qkv_w.astype(jnp.float32)).astype(jnp.bfloat16)
        key_cache = lax.dynamic_update_index_in_dim(key_cache, projected[:, :, 1], patch_id, 1)
        value_cache = lax.dynamic_update_index_in_dim(value_cache, projected[:, :, 2], patch_id, 1)
        attended = attend(projected[:, :, 0].reshape(requests, PTOK, HEADS, HD), key_cache.reshape(requests, SEQ, HEADS, HD), value_cache.reshape(requests, SEQ, HEADS, HD), valid_keys).reshape(requests, PTOK, D)
        after_attn = tokens_in + gate_attn * grouped_sum(attended, out_w)
        normed_mlp = (layer_norm(after_attn) * (1.0 + scale_mlp) + shift_mlp).astype(jnp.bfloat16)
        hidden = jax.nn.gelu(jnp.einsum('rtd,df->rtf', normed_mlp.astype(jnp.float32), up_w.astype(jnp.float32)), approximate=True).astype(jnp.bfloat16)
        result = (after_attn + gate_mlp * grouped_sum(hidden, down_w)).astype(jnp.bfloat16)
        results = lax.dynamic_update_index_in_dim(results, result, patch_id, 1)
    return results

def reference(latents, timesteps, lengths, patch_order, ada_weight, qkv_weight, out_weight, up_weight, down_weight, stale_keys, stale_values):
    cond = jax.nn.silu(sinusoid(timesteps)).astype(jnp.bfloat16)
    valid_keys = jnp.arange(SEQ, dtype=jnp.int32)[None, :] < lengths[:, None]
    first = run_section(latents, cond, ada_weight[0], qkv_weight[0], out_weight[0], up_weight[0], down_weight[0], stale_keys[0], stale_values[0], valid_keys, patch_order)
    second = run_section(first, cond, ada_weight[1], qkv_weight[1], out_weight[1], up_weight[1], down_weight[1], stale_keys[1], stale_values[1], valid_keys, patch_order)
    return jnp.stack([first, second])
```

```python
import functools
import math

import jax
import jax.numpy as jnp
from jax import lax
from jax.experimental import pallas as pl
from jax.experimental.pallas import tpu as pltpu
from jax.sharding import PartitionSpec as P

HD = 72
LANES = 128
SUBLANES = 16
SWAP = [(0, 1), (1, 0)]
VMEM_LIMIT = 48 * 1024 * 1024


def sinusoid(step_ids, width):
    half_width = width // 2
    frequency = jnp.exp(-math.log(10000.0) * jnp.arange(half_width, dtype=jnp.float32) / half_width)
    angles = step_ids.astype(jnp.float32)[:, None] * frequency[None, :]
    return jnp.concatenate([jnp.cos(angles), jnp.sin(angles)], axis=1)


def layer_norm(inputs):
    center = jnp.mean(inputs, axis=-1, keepdims=True)
    spread = jnp.mean(jnp.square(inputs - center), axis=-1, keepdims=True)
    return (inputs - center) * lax.rsqrt(spread + 1e-06)


def dot_nt(left, right):
    return lax.dot_general(left, right, (((1,), (1,)), ((), ())), preferred_element_type=jnp.float32)


def after(value, *others):
    return lax.optimization_barrier((value,) + others)[0]


class Ring:
    def __init__(self):
        self.core = lax.axis_index("section")
        self.size = lax.axis_size("row")
        self.order = list(range(0, self.size, 2)) + list(range(self.size - 1, 0, -2))
        n, order = self.size, self.order
        self.pairs = [(order[i], order[(i + 1) % n]) for i in range(n)]
        self.pairs += [(n + order[(i + 1) % n], n + order[i]) for i in range(n)]

    def owner(self, hop):
        place = [0] * self.size
        for i, r in enumerate(self.order):
            place[r] = i
        here = jnp.asarray(place, jnp.int32)[lax.axis_index("row")]
        return jnp.asarray(self.order, jnp.int32)[(here - hop) % self.size]

    def half_rows(self, rows):
        half = (rows + 1) // 2
        if rows % SUBLANES == 0:
            half = -(-half // SUBLANES) * SUBLANES
        return half

    def gather(self, shard):
        rows = shard.shape[0]
        half = self.half_rows(rows)
        parts = [shard]
        held = shard
        for hop in range(1, self.size // 2 + 1):
            if hop == self.size // 2:
                held = jnp.where(self.core == 0, held[:half], held[rows - half:])
            held = lax.ppermute(held, ("section", "row"), self.pairs)
            parts += [held, lax.ppermute(held, "section", SWAP)]
        return parts

    def places(self, rows):
        half = self.half_rows(rows)
        back = jnp.where(self.core == 0, 1, -1)
        out = [(rows, 0, self.owner(0) * rows)]
        for hop in range(1, self.size // 2 + 1):
            near, far = self.owner(hop * back) * rows, self.owner(-hop * back) * rows
            if hop < self.size // 2:
                out += [(rows, 0, near), (rows, 0, far)]
            else:
                rest = rows - half
                out += [
                    (half, 0, near + jnp.where(self.core == 0, 0, rest)),
                    (rest, jnp.where(self.core == 0, half - rest, 0), far + jnp.where(self.core == 0, half, 0)),
                ]
        return out


class Weights:
    def __init__(self, ring, rows):
        self.total = rows * ring.size
        self.spots = ring.places(rows)
        self.direct = rows % SUBLANES == 0
        if self.direct:
            self.counts = [spot[0] for spot in self.spots]
            self.meta = jnp.stack([jnp.asarray(v, jnp.int32) for spot in self.spots for v in spot[1:]])
        else:
            self.counts = [self.total]
            self.meta = jnp.zeros((2,), jnp.int32)

    def lay(self, parts):
        if self.direct:
            return parts
        whole = jnp.zeros((self.total, parts[0].shape[1]), parts[0].dtype)
        for part, (count, first, place) in zip(parts, self.spots):
            block = lax.dynamic_slice_in_dim(part, first, count, 0)
            whole = lax.dynamic_update_slice_in_dim(whole, block, place, 0)
        return [whole]


def weight_copies(meta_ref, refs, counts, columns, buffer, sems):
    copies = []
    for i, (ref, count) in enumerate(zip(refs, counts)):
        first = pl.multiple_of(meta_ref[2 * i], SUBLANES)
        place = pl.multiple_of(meta_ref[2 * i + 1], SUBLANES)
        copies.append(pltpu.make_async_copy(
            ref.at[pl.ds(first, count), columns], buffer.at[pl.ds(place, count), :], sems.at[i]))
    return copies


def modulated(x, mod_ref, shift, scale):
    return (layer_norm(x) * (1.0 + mod_ref[scale:scale + 1, :]) + mod_ref[shift:shift + 1, :]).astype(jnp.bfloat16)


def qkv_body(counts, width, first_layer, meta_ref, *refs):
    if first_layer:
        x_ref, mod_ref = refs[:2]
        refs = refs[2:]
    else:
        x1_ref, own_ref, other_ref, last_ref, mod_ref = refs[:5]
        refs = refs[5:]
    shards, refs = refs[:len(counts)], refs[len(counts):]
    if first_layer:
        q_ref, kv_ref, buffer, sems = refs
    else:
        q_ref, kv_ref, x_out_ref, buffer, sems = refs
    start = width // LANES * LANES
    copies = weight_copies(meta_ref, shards, counts, pl.ds(start, buffer.shape[1]), buffer, sems)
    for copy in copies:
        copy.start()
    if first_layer:
        x = x_ref[...].astype(jnp.float32)
    else:
        summed = own_ref[...].astype(jnp.float32) + other_ref[...].astype(jnp.float32)
        x = (x1_ref[...] + last_ref[5:6, :] * summed).astype(jnp.bfloat16)
        x_out_ref[...] = x
        x = x.astype(jnp.float32)
    h = modulated(x, mod_ref, 0, 1)
    for copy in copies:
        copy.wait()
    out = jnp.dot(h, buffer[...], preferred_element_type=jnp.float32).astype(jnp.bfloat16)
    skip = width - start
    q_ref[...] = out[:, skip:skip + width]
    kv_ref[0] = out[:, skip + width:skip + 2 * width]
    kv_ref[1] = out[:, skip + 2 * width:skip + 3 * width]


def attend_body(counts, chunk, meta_ref, info_ref, q_ref, own_refs, other_refs, stale_k, stale_v, shards,
                out_ref, k_buf, v_buf, buffer, sems, kv_sems):
    tokens, width = q_ref.shape
    heads = width // HD
    per_core = len(own_refs)
    core = info_ref[0]
    wide = buffer.shape[1]
    copies = weight_copies(meta_ref, shards, counts, pl.ds(0, wide), buffer, sems)
    patches = stale_k.shape[0]
    for patch in range(patches):
        fresh = info_ref[2 + patch] == 1
        mine = core == patch // per_core
        for which, (stale, target) in enumerate(((stale_k, k_buf), (stale_v, v_buf))):
            place = target.at[pl.ds(patch * tokens, tokens), :]
            sem = kv_sems.at[2 * patch + which]
            slot = patch % per_core

            @pl.when(fresh & mine)
            def _():
                pltpu.make_async_copy(own_refs[slot].at[which], place, sem).start()

            @pl.when(fresh & jnp.logical_not(mine))
            def _():
                pltpu.make_async_copy(other_refs[slot].at[which], place, sem).start()

            @pl.when(jnp.logical_not(fresh))
            def _():
                pltpu.make_async_copy(stale.at[patch], place, sem).start()
    for copy in copies:
        copy.start()
    for patch in range(patches):
        for which, (stale, target) in enumerate(((stale_k, k_buf), (stale_v, v_buf))):
            place = target.at[pl.ds(patch * tokens, tokens), :]
            pltpu.make_async_copy(stale.at[patch], place, kv_sems.at[2 * patch + which]).wait()
    keys = k_buf.shape[0]
    valid = lax.broadcasted_iota(jnp.int32, (1, keys), 1) < info_ref[1]
    factor = 1.0 / (math.sqrt(HD) * math.log(2.0))
    blocks = [None] * (wide // LANES)
    for head in range(heads):
        low, high = head * HD, head * HD + HD
        a = low // LANES * LANES
        b = min(-(-high // LANES) * LANES, width)
        lane = lax.broadcasted_iota(jnp.int32, (1, b - a), 1) + a
        inside = (lane >= low) & (lane < high)
        q = jnp.where(inside, q_ref[:, a:b], jnp.zeros((), jnp.bfloat16))
        scores = jnp.where(valid, dot_nt(q, k_buf[:, a:b]), -1e30)
        top = jnp.max(scores, axis=-1, keepdims=True)
        weights = jnp.exp2((scores - top) * factor)
        totals = jnp.sum(weights, axis=-1, keepdims=True)
        mixed = jnp.dot(weights.astype(jnp.bfloat16), v_buf[:, a:b], preferred_element_type=jnp.float32)
        mixed = jnp.where(inside, mixed / totals, 0.0)
        if (b - a) % LANES:
            mixed = jnp.concatenate([mixed, jnp.zeros((tokens, LANES - (b - a) % LANES), jnp.float32)], axis=1)
        for j in range(mixed.shape[1] // LANES):
            piece = mixed[:, j * LANES:(j + 1) * LANES]
            at = a // LANES + j
            blocks[at] = piece if blocks[at] is None else blocks[at] + piece
    attended = jnp.concatenate(blocks, axis=1).astype(jnp.bfloat16)
    for copy in copies:
        copy.wait()
    out_ref[...] = dot_nt(attended, buffer[...]).astype(jnp.bfloat16)


def up_body(counts, meta_ref, x_ref, own_ref, other_ref, mod_ref, *refs):
    shards, (x1_ref, g_ref, buffer, sems) = refs[:len(counts)], refs[len(counts):]
    copies = weight_copies(meta_ref, shards, counts, pl.ds(0, buffer.shape[1]), buffer, sems)
    for copy in copies:
        copy.start()
    summed = own_ref[...].astype(jnp.float32) + other_ref[...].astype(jnp.float32)
    x1 = x_ref[...].astype(jnp.float32) + mod_ref[2:3, :] * summed
    x1_ref[...] = x1
    h = modulated(x1, mod_ref, 3, 4)
    for copy in copies:
        copy.wait()
    hidden = jnp.dot(h, buffer[...], preferred_element_type=jnp.float32)
    g_ref[...] = jax.nn.gelu(hidden, approximate=True).astype(jnp.bfloat16)


def down_body(counts, meta_ref, g_ref, *refs):
    shards, (out_ref, buffer, sems) = refs[:len(counts)], refs[len(counts):]
    copies = weight_copies(meta_ref, shards, counts, pl.ds(0, buffer.shape[1]), buffer, sems)
    for copy in copies:
        copy.start()
    for copy in copies:
        copy.wait()
    out_ref[...] = dot_nt(g_ref[...], buffer[...]).astype(jnp.bfloat16)


IN_SMEM = pl.BlockSpec(memory_space=pltpu.SMEM)
IN_VMEM = pl.BlockSpec(memory_space=pltpu.VMEM)
IN_HBM = pl.BlockSpec(memory_space=pl.ANY)


def call(body, name, args, specs, outs, scratch, flops):
    return pl.pallas_call(
        body,
        name=name,
        out_shape=outs,
        in_specs=specs,
        out_specs=[IN_VMEM] * len(outs),
        scratch_shapes=scratch,
        compiler_params=pltpu.CompilerParams(vmem_limit_bytes=VMEM_LIMIT),
        cost_estimate=pl.CostEstimate(flops=flops, bytes_accessed=8 << 20, transcendentals=0),
    )(*args)


def shape_of(*dims, dtype=jnp.bfloat16):
    return jax.ShapeDtypeStruct(dims, dtype)


def modulations(timesteps, ada_local):
    rows, kinds, columns = ada_local.shape
    steps = lax.all_gather(timesteps, "row", axis=0, tiled=True)
    width = rows * lax.axis_size("row")
    cond = jax.nn.silu(sinusoid(steps, width)).astype(jnp.bfloat16)
    cond = lax.dynamic_slice_in_dim(cond, lax.axis_index("row") * rows, rows, 1)
    part = jnp.einsum("rd,dkc->rkc", cond, ada_local, preferred_element_type=jnp.float32)
    summed = lax.psum_scatter(part, "row", scatter_dimension=0, tiled=True)[0]
    mine = lax.all_gather(summed, "col", axis=1, tiled=True)
    other = lax.ppermute(mine, "section", SWAP)
    core = lax.axis_index("section")
    return [jnp.where(core == s, mine, other) for s in range(2)]


def local(
    latents,
    timesteps,
    lengths,
    patch_order,
    ada_weight,
    qkv_weight,
    out_weight,
    up_weight,
    down_weight,
    stale_keys,
    stale_values,
):
    core = lax.axis_index("section")
    col = lax.axis_index("col")
    ring = Ring()
    patches, shared_tokens, depth = latents.shape[1:]
    tokens = shared_tokens * 2
    per_core = patches // 2
    width = qkv_weight.shape[3]
    hidden = up_weight.shape[2]
    rows = qkv_weight.shape[1]
    wide = -(-width // LANES) * LANES

    pieces = [
        jnp.concatenate([out_weight[0].T, qkv_weight[0].reshape(rows, 3 * width)], axis=1),
        up_weight[0],
        down_weight[0].T,
    ]
    shards = [[], []]
    for piece in pieces:
        other = lax.ppermute(piece, "section", SWAP)
        for s in range(2):
            shards[s].append(jnp.where(core == s, piece, other))
    stale = [[], []]
    for cache in (stale_keys[0, 0], stale_values[0, 0]):
        other = lax.ppermute(cache, "section", SWAP)
        for s in range(2):
            stale[s].append(jnp.where(core == s, cache, other))

    first_patch = core * per_core
    own_half = lax.dynamic_slice_in_dim(latents[0], first_patch, per_core, 0)
    x_chunks = []
    for i in range(per_core):
        other = lax.ppermute(own_half[i], "col", SWAP)
        x_chunks.append(jnp.where(col == 0, jnp.concatenate([own_half[i], other]), jnp.concatenate([other, own_half[i]])))

    mods = modulations(timesteps, ada_weight[0])

    gathered = [[], []]
    previous = []
    for s in range(2):
        for shard in shards[s]:
            if previous:
                shard = after(shard, previous[-1])
            parts = ring.gather(shard)
            previous.append(parts[-4])
            gathered[s].append(parts)
    layout = Weights(ring, rows)
    counts = layout.counts
    gathered = [[layout.lay(parts) for parts in section] for section in gathered]
    n_parts = len(counts)
    weight_specs = [IN_HBM] * n_parts

    place = jnp.argsort(patch_order)
    position = lax.dynamic_slice_in_dim(place, first_patch, per_core, 0)
    fresh = (place[None, :] <= position[:, None]).astype(jnp.int32)
    infos = [
        jnp.concatenate([core.astype(jnp.int32)[None], lengths.astype(jnp.int32), fresh[i]])
        for i in range(per_core)
    ]

    def weight_buffers(columns):
        return [pltpu.VMEM((layout.total, columns), jnp.bfloat16), pltpu.SemaphoreType.DMA((n_parts,))]

    finished = []
    carried = None
    for s in range(2):
        mod = mods[s]
        first, up_parts, down_parts = gathered[s]
        queries, fresh_own, fresh_other = [], [], []
        start = width // LANES * LANES
        for i in range(per_core):
            outs = [shape_of(tokens, width), shape_of(2, tokens, width)]
            if s == 0:
                args, specs = [x_chunks[i], mod], [IN_VMEM] * 2
            else:
                x1, own, other = carried[i]
                args, specs = [x1, own, other, mods[0], mod], [IN_VMEM] * 5
                outs.append(shape_of(tokens, depth))
            result = call(
                functools.partial(qkv_body, counts, width, s == 0), "qkv",
                [layout.meta] + args + first, [IN_SMEM] + specs + weight_specs, outs,
                weight_buffers(width + 3 * width - start), 2 * tokens * depth * 3 * width)
            if s == 1:
                x_chunks[i] = result[2]
            queries.append(result[0])
            fresh_own.append(result[1])
            fresh_other.append(lax.ppermute(result[1], "section", SWAP))
        if s == 1:
            finished.append([
                lax.dynamic_slice_in_dim(x, col * shared_tokens, shared_tokens, 0) for x in x_chunks])
        sums = []
        for i in range(per_core):
            part = call(
                functools.partial(attend_kernel, counts, per_core), "attend",
                [layout.meta, infos[i], queries[i]] + fresh_own + fresh_other + stale[s] + first,
                [IN_SMEM, IN_SMEM, IN_VMEM] + [IN_HBM] * (2 * per_core + 2) + weight_specs,
                [shape_of(tokens, depth)],
                [pltpu.VMEM((patches * tokens, width), jnp.bfloat16)] * 2 + weight_buffers(wide)
                + [pltpu.SemaphoreType.DMA((2 * patches,))],
                4 * tokens * patches * tokens * width + 2 * tokens * depth * width)[0]
            sums.append((part, lax.ppermute(part, "col", SWAP)))
        carried = []
        for i in range(per_core):
            own, other = sums[i]
            x1, g = call(
                functools.partial(up_body, counts), "up",
                [layout.meta, x_chunks[i], own, other, mod] + up_parts,
                [IN_SMEM] + [IN_VMEM] * 4 + weight_specs,
                [shape_of(tokens, depth, dtype=jnp.float32), shape_of(tokens, hidden)],
                weight_buffers(hidden), 2 * tokens * depth * hidden)
            part = call(
                functools.partial(down_body, counts), "down",
                [layout.meta, g] + down_parts, [IN_SMEM, IN_VMEM] + weight_specs,
                [shape_of(tokens, depth)], weight_buffers(hidden), 2 * tokens * depth * hidden)[0]
            if s == 0:
                carried.append((x1, part, lax.ppermute(part, "col", SWAP)))
            else:
                away = lax.dynamic_slice_in_dim(part, (1 - col) * shared_tokens, shared_tokens, 0)
                other = lax.ppermute(away, "col", SWAP)
                kept = lax.dynamic_slice_in_dim(part, col * shared_tokens, shared_tokens, 0)
                x1 = lax.dynamic_slice_in_dim(x1, col * shared_tokens, shared_tokens, 0)
                summed = kept.astype(jnp.float32) + other.astype(jnp.float32)
                carried.append((x1 + mod[5][None, :] * summed).astype(jnp.bfloat16))
    finished.append(carried)

    done = [jnp.stack(chunks) for chunks in finished]
    kept = jnp.where(core == 0, done[0], done[1])
    came = lax.ppermute(jnp.where(core == 0, done[1], done[0]), "section", SWAP)
    result = jnp.where(core == 0, jnp.concatenate([kept, came]), jnp.concatenate([came, kept]))
    return result[None, None]


def attend_kernel(counts, per_core, meta_ref, info_ref, q_ref, *refs):
    own, refs = refs[:per_core], refs[per_core:]
    other, refs = refs[:per_core], refs[per_core:]
    (stale_k, stale_v), refs = refs[:2], refs[2:]
    shards, refs = refs[:len(counts)], refs[len(counts):]
    attend_body(counts, per_core, meta_ref, info_ref, q_ref, own, other, stale_k, stale_v, shards, *refs)


def solution(mesh):
    return jax.shard_map(
        local,
        mesh=mesh,
        in_specs=(
            P("row", None, "col", None),
            P("row"),
            P("row"),
            P(),
            P("section", "row", None, "col"),
            P("section", "row", None, "col"),
            P("section", "col", "row"),
            P("section", "row", "col"),
            P("section", "col", "row"),
            P("section", "row", None, None, "col"),
            P("section", "row", None, None, "col"),
        ),
        out_specs=P("section", "row", None, "col", None),
        check_vma=False,
    )
```

```python
import functools
import math

import jax
import jax.numpy as jnp
from jax import lax
from jax.experimental import pallas as pl
from jax.experimental.pallas import tpu as pltpu
from jax.sharding import PartitionSpec as P

HD = 72
LANES = 128
SUBLANES = 16
SWAP = [(0, 1), (1, 0)]
VMEM_LIMIT = 62 * 1024 * 1024


def sinusoid(step_ids, width):
    half_width = width // 2
    frequency = jnp.exp(-math.log(10000.0) * jnp.arange(half_width, dtype=jnp.float32) / half_width)
    angles = step_ids.astype(jnp.float32)[:, None] * frequency[None, :]
    return jnp.concatenate([jnp.cos(angles), jnp.sin(angles)], axis=1)


def layer_norm(inputs):
    center = jnp.mean(inputs, axis=-1, keepdims=True)
    spread = jnp.mean(jnp.square(inputs - center), axis=-1, keepdims=True)
    return (inputs - center) * lax.rsqrt(spread + 1e-06)


def dot_nt(left, right):
    return lax.dot_general(left, right, (((1,), (1,)), ((), ())), preferred_element_type=jnp.float32)


def after(value, *others):
    return lax.optimization_barrier((value,) + others)[0]


def place_of(row, size):
    half = lax.div(row, 2)
    return jnp.where(lax.rem(row, 2) == 0, half, size - 1 - half)


def row_at(place, size):
    place = lax.rem(place + size, size)
    return jnp.where(place < size // 2, 2 * place, 2 * (size - 1 - place) + 1)


def half_rows(rows):
    half = (rows + 1) // 2
    if rows % SUBLANES == 0:
        half = -(-half // SUBLANES) * SUBLANES
    return half


def spots(core, row, size, rows):
    half = half_rows(rows)
    rest = rows - half
    here = place_of(row, size)
    back = jnp.where(core == 0, 1, -1)
    out = [(rows, 0, row * rows)]
    for hop in range(1, size // 2 + 1):
        near = row_at(here - hop * back, size) * rows
        far = row_at(here + hop * back, size) * rows
        if hop < size // 2:
            out += [(rows, 0, near), (rows, 0, far)]
        else:
            out += [
                (half, 0, near + jnp.where(core == 0, 0, rest)),
                (rest, jnp.where(core == 0, half - rest, 0), far + jnp.where(core == 0, half, 0)),
            ]
    return out


class Ring:
    def __init__(self, rows):
        self.core = lax.axis_index("section")
        self.size = lax.axis_size("row")
        self.rows = rows
        n = self.size
        order = list(range(0, n, 2)) + list(range(n - 1, 0, -2))
        self.pairs = [(order[i], order[(i + 1) % n]) for i in range(n)]
        self.pairs += [(n + order[(i + 1) % n], n + order[i]) for i in range(n)]
        self.hops = n // 2
        self.direct = rows % SUBLANES == 0
        if self.direct:
            self.counts = [spot[0] for spot in spots(0, 0, n, rows)]
        else:
            self.counts = [rows * n]

    def hop(self, number, held):
        if number == self.hops:
            half = half_rows(self.rows)
            held = jnp.where(self.core == 0, held[:half], held[self.rows - half:])
        held = lax.ppermute(held, ("section", "row"), self.pairs)
        return held, lax.ppermute(held, "section", SWAP)

    def lay(self, parts):
        if self.direct:
            return parts
        total = self.rows * self.size
        whole = jnp.zeros((total, parts[0].shape[1]), parts[0].dtype)
        for part, spot in zip(parts, spots(self.core, lax.axis_index("row"), self.size, self.rows)):
            block = lax.dynamic_slice_in_dim(part, spot[1], spot[0], 0)
            whole = lax.dynamic_update_slice_in_dim(whole, block, spot[2], 0)
        return [whole]


def weight_copies(where_ref, size, refs, first_column, buffer, sems):
    tiles = sems.shape[1]
    total, wide = buffer.shape
    step = wide // tiles
    rows = total // size
    if len(refs) == 1:
        places = [(total, 0, 0)]
    else:
        places = spots(where_ref[0], where_ref[1], size, rows)
    out = []
    for tile in range(tiles):
        copies = []
        for i, (ref, (count, first, place)) in enumerate(zip(refs, places)):
            if not isinstance(first, int):
                first = pl.multiple_of(first, SUBLANES)
            if not isinstance(place, int):
                place = pl.multiple_of(place, SUBLANES)
            copies.append(pltpu.make_async_copy(
                ref.at[pl.ds(first, count), pl.ds(first_column + tile * step, step)],
                buffer.at[pl.ds(place, count), pl.ds(tile * step, step)], sems.at[i, tile]))
        out.append(copies)
    for copies in out:
        for copy in copies:
            copy.start()
    return out


def wait_all(copies):
    for copy in copies:
        copy.wait()


def modulated(x, mod_ref, shift, scale):
    return (layer_norm(x) * (1.0 + mod_ref[scale:scale + 1, :]) + mod_ref[shift:shift + 1, :]).astype(jnp.bfloat16)


def qkv_body(size, n_parts, width, chunks, first_layer, where_ref, *refs):
    if first_layer:
        x_refs, mod_ref, refs = refs[:chunks], refs[chunks], refs[chunks + 1:]
    else:
        x1_ref, own_ref, other_ref, last_ref, mod_ref = refs[:5]
        refs = refs[5:]
    shards, refs = refs[:n_parts], refs[n_parts:]
    q_ref, kv_ref = refs[:2]
    buffer, sems = refs[-2:]
    start = width // LANES * LANES
    copies = weight_copies(where_ref, size, shards, start, buffer, sems)
    if first_layer:
        x = jnp.concatenate([ref[...] for ref in x_refs], axis=0).astype(jnp.float32)
    else:
        summed = own_ref[...].astype(jnp.float32) + other_ref[...].astype(jnp.float32)
        x = (x1_ref[...] + last_ref[5:6, :] * summed).astype(jnp.bfloat16)
        refs[2][...] = x
        x = x.astype(jnp.float32)
    h = modulated(x, mod_ref, 0, 1)
    outs = []
    step = buffer.shape[1] // len(copies)
    for tile, waits in enumerate(copies):
        wait_all(waits)
        weight = buffer[:, tile * step:(tile + 1) * step]
        outs.append(jnp.dot(h, weight, preferred_element_type=jnp.float32).astype(jnp.bfloat16))
    out = jnp.concatenate(outs, axis=1)
    skip = width - start
    tokens = x.shape[0] // chunks
    for i in range(chunks):
        part = out[i * tokens:(i + 1) * tokens]
        q_ref[i] = part[:, skip:skip + width]
        for which in range(2):
            low = skip + (1 + which) * width
            kv_ref[i, which] = part[:, low:low + width].T


def attend_body(size, n_parts, section, chunk, per_core, where_ref, order_ref, length_ref, q_ref, own_ref, other_ref, *refs):
    stale, refs = refs[:4], refs[4:]
    shards, refs = refs[:n_parts], refs[n_parts:]
    out_ref, k_buf, v_buf, buffer, sems, kv_sems = refs
    tokens, width = q_ref.shape[1:]
    heads = width // HD
    core = where_ref[0]
    wide = buffer.shape[1]
    patches = stale[0].shape[0]
    here = core * per_core + chunk
    positions = [sum(jnp.where(order_ref[j] == p, j, 0) for j in range(patches)) for p in range(patches)]
    position = sum(jnp.where(here == p, positions[p], 0) for p in range(patches))
    for patch in range(patches):
        fresh = positions[patch] <= position
        mine = core == patch // per_core
        slot = patch % per_core
        for which, target in enumerate((k_buf, v_buf)):
            place = target.at[:, pl.ds(patch * tokens, tokens)]
            sem = kv_sems.at[2 * patch + which]
            sources = [
                (fresh & mine, own_ref.at[slot, which]),
                (fresh & jnp.logical_not(mine), other_ref.at[slot, which]),
                (jnp.logical_not(fresh) & (core == section), stale[which].at[patch]),
                (jnp.logical_not(fresh) & (core != section), stale[2 + which].at[patch]),
            ]
            for condition, source in sources:
                @pl.when(condition)
                def _(source=source, place=place, sem=sem):
                    pltpu.make_async_copy(source, place, sem).start()
    copies = weight_copies(where_ref, size, shards, 0, buffer, sems)
    for patch in range(patches):
        for which, target in enumerate((k_buf, v_buf)):
            place = target.at[:, pl.ds(patch * tokens, tokens)]
            pltpu.make_async_copy(stale[which].at[patch], place, kv_sems.at[2 * patch + which]).wait()
    keys = k_buf.shape[1]
    valid = lax.broadcasted_iota(jnp.int32, (1, keys), 1) < length_ref[0]
    factor = 1.0 / (math.sqrt(HD) * math.log(2.0))
    blocks = [None] * (wide // LANES)
    for head in range(heads):
        low, high = head * HD, head * HD + HD
        a = low // LANES * LANES
        b = min(-(-high // LANES) * LANES, width)
        lane = lax.broadcasted_iota(jnp.int32, (1, b - a), 1) + a
        inside = (lane >= low) & (lane < high)
        q = jnp.where(inside, q_ref[0, :, a:b], jnp.zeros((), jnp.bfloat16))
        scores = jnp.dot(q, k_buf[a:b, :], preferred_element_type=jnp.float32)
        scores = jnp.where(valid, scores, -1e30)
        top = jnp.max(scores, axis=-1, keepdims=True)
        weights = jnp.exp2((scores - top) * factor)
        totals = jnp.sum(weights, axis=-1, keepdims=True)
        mixed = dot_nt(weights.astype(jnp.bfloat16), v_buf[a:b, :])
        mixed = jnp.where(inside, mixed / totals, 0.0)
        if (b - a) % LANES:
            mixed = jnp.concatenate([mixed, jnp.zeros((tokens, LANES - (b - a) % LANES), jnp.float32)], axis=1)
        for j in range(mixed.shape[1] // LANES):
            piece = mixed[:, j * LANES:(j + 1) * LANES]
            at = a // LANES + j
            blocks[at] = piece if blocks[at] is None else blocks[at] + piece
    attended = jnp.concatenate(blocks, axis=1).astype(jnp.bfloat16)
    wait_all(copies[0])
    out_ref[...] = dot_nt(attended, buffer[...]).astype(jnp.bfloat16)


def up_body(size, n_parts, where_ref, x_ref, own_ref, other_ref, mod_ref, *refs):
    shards, (x1_ref, g_ref, buffer, sems) = refs[:n_parts], refs[n_parts:]
    copies = weight_copies(where_ref, size, shards, 0, buffer, sems)
    summed = own_ref[...].astype(jnp.float32) + other_ref[...].astype(jnp.float32)
    x1 = x_ref[...].astype(jnp.float32) + mod_ref[2:3, :] * summed
    x1_ref[...] = x1
    h = modulated(x1, mod_ref, 3, 4)
    step = buffer.shape[1] // len(copies)
    for tile, waits in enumerate(copies):
        wait_all(waits)
        columns = slice(tile * step, (tile + 1) * step)
        hidden = jnp.dot(h, buffer[:, columns], preferred_element_type=jnp.float32)
        g_ref[:, columns] = jax.nn.gelu(hidden, approximate=True).astype(jnp.bfloat16)


def down_body(size, n_parts, where_ref, g_ref, *refs):
    shards, (out_ref, buffer, sems) = refs[:n_parts], refs[n_parts:]
    copies = weight_copies(where_ref, size, shards, 0, buffer, sems)
    step = buffer.shape[1] // len(copies)
    total = None
    for tile, waits in enumerate(copies):
        wait_all(waits)
        columns = slice(tile * step, (tile + 1) * step)
        part = dot_nt(g_ref[:, columns], buffer[:, columns])
        total = part if total is None else total + part
    out_ref[...] = total.astype(jnp.bfloat16)


IN_SMEM = pl.BlockSpec(memory_space=pltpu.SMEM)
IN_VMEM = pl.BlockSpec(memory_space=pltpu.VMEM)
IN_HBM = pl.BlockSpec(memory_space=pl.ANY)


def call(body, name, args, specs, outs, scratch, flops):
    return pl.pallas_call(
        body,
        name=name,
        out_shape=outs,
        in_specs=specs,
        out_specs=[IN_VMEM] * len(outs),
        scratch_shapes=scratch,
        compiler_params=pltpu.CompilerParams(vmem_limit_bytes=VMEM_LIMIT),
        cost_estimate=pl.CostEstimate(flops=flops, bytes_accessed=8 << 20, transcendentals=0),
    )(*args)


def shape_of(*dims, dtype=jnp.bfloat16):
    return jax.ShapeDtypeStruct(dims, dtype)


def partners(bit):
    return [(i, i ^ (1 << bit)) for i in range(lax.axis_size("row"))]


def all_steps(timesteps):
    n = lax.axis_size("row")
    if n & (n - 1):
        return lax.all_gather(timesteps, "row", axis=0, tiled=True)
    mine = jnp.arange(n) == lax.axis_index("row")
    steps = jnp.where(mine, timesteps, 0)
    for bit in range(n.bit_length() - 1):
        steps = steps + lax.ppermute(steps, "row", partners(bit))
    return steps


def row_sums(part):
    n = lax.axis_size("row")
    if n & (n - 1):
        return lax.psum_scatter(part, "row", scatter_dimension=0, tiled=True)[0]
    for bit in reversed(range(n.bit_length() - 1)):
        half = part.shape[0] // 2
        high = (lax.axis_index("row") >> bit) & 1
        kept = jnp.where(high == 1, part[half:], part[:half])
        away = jnp.where(high == 1, part[:half], part[half:])
        part = kept + lax.ppermute(away, "row", partners(bit))
    return part[0]


def modulation_parts(steps, ada_local):
    rows = ada_local.shape[0]
    cond = jax.nn.silu(sinusoid(steps, rows * lax.axis_size("row"))).astype(jnp.bfloat16)
    cond = lax.dynamic_slice_in_dim(cond, lax.axis_index("row") * rows, rows, 1)
    return jnp.einsum("rd,dkc->rkc", cond, ada_local, preferred_element_type=jnp.float32)


def both_modulations(summed):
    col, core = lax.axis_index("col"), lax.axis_index("section")
    other = lax.ppermute(summed, "col", SWAP)
    mine = jnp.where(col == 0, jnp.concatenate([summed, other], 1), jnp.concatenate([other, summed], 1))
    other = lax.ppermute(mine, "section", SWAP)
    return [jnp.where(core == s, mine, other) for s in range(2)]


def local(
    latents,
    timesteps,
    lengths,
    patch_order,
    ada_weight,
    qkv_weight,
    out_weight,
    up_weight,
    down_weight,
    stale_keys,
    stale_values,
):
    core = lax.axis_index("section")
    col = lax.axis_index("col")
    patches, shared_tokens, depth = latents.shape[1:]
    tokens = shared_tokens * 2
    per_core = patches // 2
    width = qkv_weight.shape[3]
    hidden = up_weight.shape[2]
    rows = qkv_weight.shape[1]
    wide = -(-width // LANES) * LANES
    ring = Ring(rows)
    size = ring.size
    n_parts = len(ring.counts)
    where = jnp.stack([core, lax.axis_index("row")]).astype(jnp.int32)

    def cores_shards(piece):
        other = lax.ppermute(piece, "section", SWAP)
        return [jnp.where(core == s, piece, other) for s in range(2)]

    first_piece = jnp.concatenate([out_weight[0].T, qkv_weight[0].reshape(rows, 3 * width)], axis=1)
    pieces = [cores_shards(first_piece)]

    first_patch = core * per_core
    own_half = lax.dynamic_slice_in_dim(latents[0], first_patch, per_core, 0)
    x_chunks = []
    for i in range(per_core):
        other = lax.ppermute(own_half[i], "col", SWAP)
        x_chunks.append(jnp.where(col == 0, jnp.concatenate([own_half[i], other]), jnp.concatenate([other, own_half[i]])))

    class Travel:
        def __init__(self, shard):
            self.held, self.parts, self.done = shard, [shard], 0

        def go(self, *gates):
            if gates:
                self.held = after(self.held, *gates)
            for _ in range(ring.hops // 4):
                self.done += 1
                self.held, other = ring.hop(self.done, self.held)
                self.parts += [self.held, other]
            return self.held

        def laid(self):
            return ring.lay(self.parts)

    first = Travel(pieces[0][0])
    steps = all_steps(after(timesteps, first.held))
    hop1 = first.go()
    summed = row_sums(modulation_parts(after(steps, hop1), ada_weight[0]))
    hop2 = first.go()
    for piece in (up_weight[0], down_weight[0].T):
        pieces.append(cores_shards(after(piece, hop1)))
    mods = both_modulations(after(summed, hop2))
    hop3 = first.go(summed, x_chunks[0])
    stale = [jnp.swapaxes(cache, 1, 2) for cache in (stale_keys[0, 0], stale_values[0, 0])]
    stale += [lax.ppermute(after(cache, hop1), "section", SWAP) for cache in stale]
    second, third = Travel(pieces[1][0]), Travel(pieces[2][0])
    hop4 = first.go(*mods, x_chunks[1])
    second.go(hop3)
    second.go(hop4)
    third.go(second.parts[1])

    weight_specs = [IN_HBM] * n_parts

    def weight_buffers(columns, tiles):
        return [pltpu.VMEM((rows * size, columns), jnp.bfloat16), pltpu.SemaphoreType.DMA((n_parts, tiles))]

    def project(s, chunks, args, shards):
        start = width // LANES * LANES
        outs = [shape_of(chunks, tokens, width), shape_of(chunks, 2, width, tokens)]
        if s == 1:
            outs.append(shape_of(tokens, depth))
        return call(
            functools.partial(qkv_body, size, n_parts, width, chunks, s == 0), "qkv",
            [where] + args + shards, [IN_SMEM] + [IN_VMEM] * len(args) + weight_specs, outs,
            weight_buffers(4 * width - start, 2), 2 * chunks * tokens * depth * 3 * width)

    def attend(s, i, query, fresh_own, fresh_other, shards):
        return call(
            functools.partial(attend_body, size, n_parts, s, i, per_core), "attend",
            [where, patch_order, lengths, query, fresh_own, fresh_other] + stale + shards,
            [IN_SMEM] * 3 + [IN_VMEM] + [IN_HBM] * 6 + weight_specs,
            [shape_of(tokens, depth)],
            [pltpu.VMEM((width, patches * tokens), jnp.bfloat16)] * 2 + weight_buffers(wide, 1)
            + [pltpu.SemaphoreType.DMA((2 * patches,))],
            4 * tokens * patches * tokens * width + 2 * tokens * depth * width)[0]

    def mlp_up(x, own, other, mod, shards):
        return call(
            functools.partial(up_body, size, n_parts), "up",
            [where, x, own, other, mod] + shards,
            [IN_SMEM] + [IN_VMEM] * 4 + weight_specs,
            [shape_of(tokens, depth, dtype=jnp.float32), shape_of(tokens, hidden)],
            weight_buffers(hidden, 3), 2 * tokens * depth * hidden)

    def mlp_down(g, shards):
        return call(
            functools.partial(down_body, size, n_parts), "down",
            [where, g] + shards, [IN_SMEM, IN_VMEM] + weight_specs,
            [shape_of(tokens, depth)], weight_buffers(hidden, 3), 2 * tokens * depth * hidden)[0]

    def col_half(x):
        return lax.dynamic_slice_in_dim(x, col * shared_tokens, shared_tokens, 0)

    shards = first.laid()
    queries, fresh_own = project(0, per_core, x_chunks + [mods[0]], shards)
    fresh_other = lax.ppermute(fresh_own, "section", SWAP)
    second.go(queries)
    third.go(queries)
    att = [None] * 2
    att[0] = attend(0, 0, queries[0:1], fresh_own, fresh_other, shards)
    att_other = [lax.ppermute(att[0], "col", SWAP)]
    second.go(att[0])
    third.go(att[0])
    first = Travel(pieces[0][1])
    first.go(att[0], second.parts[5])
    att[1] = attend(0, 1, queries[1:2], fresh_own, fresh_other, shards)
    att_other.append(lax.ppermute(att[1], "col", SWAP))
    third.go(att[1])
    first.go(att[1])
    up_shards = second.laid()
    x1, g, down, down_other = [None] * 2, [None] * 2, [None] * 2, [None] * 2
    x1[0], g[0] = mlp_up(x_chunks[0], att[0], att_other[0], mods[0], up_shards)
    first.go(g[0], third.parts[5])
    second = Travel(pieces[1][1])
    second.go(g[0], first.parts[3])
    x1[1], g[1] = mlp_up(x_chunks[1], att[1], att_other[1], mods[0], up_shards)
    first.go(g[1])
    down_shards = third.laid()
    for i in range(2):
        down[i] = mlp_down(g[i], down_shards)
        down_other[i] = lax.ppermute(down[i], "col", SWAP)
    second.go(down[0])
    second.go(down[1])

    shards = first.laid()
    results = [None] * 2
    results[0] = project(1, 1, [x1[0], down[0], down_other[0], mods[0], mods[1]], shards)
    third = Travel(pieces[2][1])
    second.go(results[0][0])
    third.go(results[0][0])
    results[1] = project(1, 1, [x1[1], down[1], down_other[1], mods[0], mods[1]], shards)
    third.go(results[1][0])
    fresh_other = jnp.concatenate([lax.ppermute(result[1], "section", SWAP) for result in results])
    fresh_own = jnp.concatenate([result[1] for result in results])
    x_chunks = [result[2] for result in results]
    finished = [[col_half(x) for x in x_chunks]]
    att[0] = attend(1, 0, results[0][0], fresh_own, fresh_other, shards)
    att_other[0] = lax.ppermute(att[0], "col", SWAP)
    third.go(att[0])
    att[1] = attend(1, 1, results[1][0], fresh_own, fresh_other, shards)
    att_other[1] = lax.ppermute(att[1], "col", SWAP)
    third.go(att[1])
    up_shards, down_shards = second.laid(), third.laid()
    carried = []
    for i in range(2):
        x1, g = mlp_up(x_chunks[i], att[i], att_other[i], mods[1], up_shards)
        part = mlp_down(g, down_shards)
        away = lax.dynamic_slice_in_dim(part, (1 - col) * shared_tokens, shared_tokens, 0)
        other = lax.ppermute(away, "col", SWAP)
        summed = col_half(part).astype(jnp.float32) + other.astype(jnp.float32)
        carried.append((col_half(x1) + mods[1][5][None, :] * summed).astype(jnp.bfloat16))
    finished.append(carried)

    done = [jnp.stack(chunks) for chunks in finished]
    kept = jnp.where(core == 0, done[0], done[1])
    came = lax.ppermute(jnp.where(core == 0, done[1], done[0]), "section", SWAP)
    result = jnp.where(core == 0, jnp.concatenate([kept, came]), jnp.concatenate([came, kept]))
    return result[None, None]


def solution(mesh):
    return jax.shard_map(
        local,
        mesh=mesh,
        in_specs=(
            P("row", None, "col", None),
            P("row"),
            P("row"),
            P(),
            P("section", "row", None, "col"),
            P("section", "row", None, "col"),
            P("section", "col", "row"),
            P("section", "row", "col"),
            P("section", "col", "row"),
            P("section", "row", None, None, "col"),
            P("section", "row", None, None, "col"),
        ),
        out_specs=P("section", "row", None, "col", None),
        check_vma=False,
    )
```

```python
import functools
import math

import jax
import jax.numpy as jnp
from jax import lax
from jax.experimental import pallas as pl
from jax.experimental.pallas import tpu as pltpu
from jax.sharding import PartitionSpec as P

HD = 72
LANES = 128
SUBLANES = 16
SWAP = [(0, 1), (1, 0)]
VMEM_LIMIT = 62 * 1024 * 1024


def sinusoid(step_ids, width):
    half_width = width // 2
    frequency = jnp.exp(-math.log(10000.0) * jnp.arange(half_width, dtype=jnp.float32) / half_width)
    angles = step_ids.astype(jnp.float32)[:, None] * frequency[None, :]
    return jnp.concatenate([jnp.cos(angles), jnp.sin(angles)], axis=1)


def layer_norm(inputs):
    center = jnp.mean(inputs, axis=-1, keepdims=True)
    spread = jnp.mean(jnp.square(inputs - center), axis=-1, keepdims=True)
    return (inputs - center) * lax.rsqrt(spread + 1e-06)


def dot_nt(left, right):
    return lax.dot_general(left, right, (((1,), (1,)), ((), ())), preferred_element_type=jnp.float32)


def after(value, *others):
    return lax.optimization_barrier((value,) + others)[0]


def place_of(row, size):
    half = lax.div(row, 2)
    return jnp.where(lax.rem(row, 2) == 0, half, size - 1 - half)


def row_at(place, size):
    place = lax.rem(place + size, size)
    return jnp.where(place < size // 2, 2 * place, 2 * (size - 1 - place) + 1)


def half_rows(rows):
    half = (rows + 1) // 2
    if rows % SUBLANES == 0:
        half = -(-half // SUBLANES) * SUBLANES
    return half


def spots(core, row, size, rows):
    half = half_rows(rows)
    rest = rows - half
    here = place_of(row, size)
    back = jnp.where(core == 0, 1, -1)
    out = [(rows, 0, row * rows)]
    for hop in range(1, size // 2 + 1):
        near = row_at(here - hop * back, size) * rows
        far = row_at(here + hop * back, size) * rows
        if hop < size // 2:
            out += [(rows, 0, near), (rows, 0, far)]
        else:
            out += [
                (half, 0, near + jnp.where(core == 0, 0, rest)),
                (rest, jnp.where(core == 0, half - rest, 0), far + jnp.where(core == 0, half, 0)),
            ]
    return out


class Ring:
    def __init__(self, rows):
        self.core = lax.axis_index("section")
        self.size = lax.axis_size("row")
        self.rows = rows
        n = self.size
        order = list(range(0, n, 2)) + list(range(n - 1, 0, -2))
        self.pairs = [(order[i], order[(i + 1) % n]) for i in range(n)]
        self.pairs += [(n + order[(i + 1) % n], n + order[i]) for i in range(n)]
        self.hops = n // 2
        self.direct = rows % SUBLANES == 0
        if self.direct:
            self.counts = [spot[0] for spot in spots(0, 0, n, rows)]
        else:
            self.counts = [rows * n]

    def hop(self, number, held):
        if number == self.hops:
            half = half_rows(self.rows)
            held = jnp.where(self.core == 0, held[:half], held[self.rows - half:])
        return lax.ppermute(held, ("section", "row"), self.pairs)

    def lay(self, parts):
        if self.direct:
            return parts
        total = self.rows * self.size
        whole = jnp.zeros((total, parts[0].shape[1]), parts[0].dtype)
        for part, spot in zip(parts, spots(self.core, lax.axis_index("row"), self.size, self.rows)):
            block = lax.dynamic_slice_in_dim(part, spot[1], spot[0], 0)
            whole = lax.dynamic_update_slice_in_dim(whole, block, spot[2], 0)
        return [whole]


def weight_copies(where_ref, size, refs, first_column, buffer, sems):
    tiles = sems.shape[1]
    total, wide = buffer.shape
    step = wide // tiles
    rows = total // size
    if len(refs) == 1:
        places = [(total, 0, 0)]
    else:
        places = spots(where_ref[0], where_ref[1], size, rows)
    out = []
    for tile in range(tiles):
        copies = []
        for i, (ref, (count, first, place)) in enumerate(zip(refs, places)):
            if not isinstance(first, int):
                first = pl.multiple_of(first, SUBLANES)
            if not isinstance(place, int):
                place = pl.multiple_of(place, SUBLANES)
            copies.append(pltpu.make_async_copy(
                ref.at[pl.ds(first, count), pl.ds(first_column + tile * step, step)],
                buffer.at[pl.ds(place, count), pl.ds(tile * step, step)], sems.at[i, tile]))
        out.append(copies)
    return out


def start_all(copies):
    for copy in copies:
        copy.start()


def wait_all(copies):
    for copy in copies:
        copy.wait()


def modulated(x, mod_ref, shift, scale):
    return (layer_norm(x) * (1.0 + mod_ref[scale:scale + 1, :]) + mod_ref[shift:shift + 1, :]).astype(jnp.bfloat16)


def qkv_body(size, n_parts, width, chunks, first_layer, where_ref, *refs):
    if first_layer:
        own_refs, other_refs, mod_ref = refs[:chunks], refs[chunks:2 * chunks], refs[2 * chunks]
        refs = refs[2 * chunks + 1:]
    else:
        x1_ref, own_ref, other_ref, last_ref, mod_ref = refs[:5]
        refs = refs[5:]
    shards, refs = refs[:n_parts], refs[n_parts:]
    q_ref, kv_refs = refs[0], refs[1:1 + 2 * chunks]
    x_refs = refs[1 + 2 * chunks:-2]
    buffer, sems = refs[-2:]
    start = width // LANES * LANES
    copies = weight_copies(where_ref, size, shards, start, buffer, sems)
    for group in copies:
        start_all(group)
    if first_layer:
        first_half = where_ref[2] == 0
        halves = []
        for own, other in zip(own_refs, other_refs):
            own, other = own[...].astype(jnp.float32), other[...].astype(jnp.float32)
            halves += [jnp.where(first_half, own, other), jnp.where(first_half, other, own)]
        x = jnp.concatenate(halves, axis=0)
        tokens = x.shape[0] // chunks
        for i in range(chunks):
            x_refs[i][...] = x[i * tokens:(i + 1) * tokens].astype(jnp.bfloat16)
    else:
        summed = own_ref[...].astype(jnp.float32) + other_ref[...].astype(jnp.float32)
        x = (x1_ref[...] + last_ref[5:6, :] * summed).astype(jnp.bfloat16)
        x_refs[0][...] = x
        x = x.astype(jnp.float32)
    h = modulated(x, mod_ref, 0, 1)
    outs = []
    step = buffer.shape[1] // len(copies)
    for tile, waits in enumerate(copies):
        wait_all(waits)
        weight = buffer[:, tile * step:(tile + 1) * step]
        outs.append(jnp.dot(h, weight, preferred_element_type=jnp.float32).astype(jnp.bfloat16))
    out = jnp.concatenate(outs, axis=1)
    skip = width - start
    tokens = x.shape[0] // chunks
    for i in range(chunks):
        part = out[i * tokens:(i + 1) * tokens]
        q_ref[i] = part[:, skip:skip + width]
        for which in range(2):
            low = skip + (1 + which) * width
            kv_refs[2 * i + which][...] = part[:, low:low + width].T


def attend_body(size, n_parts, section, chunk, per_core, where_ref, order_ref, length_ref, q_ref, *refs):
    own, other, stale = refs[:2 * per_core], refs[2 * per_core:4 * per_core], refs[4 * per_core:4 * per_core + 4]
    refs = refs[4 * per_core + 4:]
    shards, refs = refs[:n_parts], refs[n_parts:]
    out_ref, k_buf, v_buf, buffer, sems, kv_sems = refs
    query = q_ref[0 if q_ref.shape[0] == 1 else chunk]
    tokens, width = query.shape
    heads = width // HD
    core = where_ref[0]
    wide = buffer.shape[1]
    patches = stale[0].shape[0]
    here = core * per_core + chunk
    positions = [sum(jnp.where(order_ref[j] == p, j, 0) for j in range(patches)) for p in range(patches)]
    position = sum(jnp.where(here == p, positions[p], 0) for p in range(patches))
    for patch in range(patches):
        fresh = positions[patch] <= position
        mine = core == patch // per_core
        slot = patch % per_core
        for which, target in enumerate((k_buf, v_buf)):
            place = target.at[:, pl.ds(patch * tokens, tokens)]
            sem = kv_sems.at[2 * patch + which]
            sources = [
                (fresh & mine, own[2 * slot + which]),
                (fresh & jnp.logical_not(mine), other[2 * slot + which]),
                (jnp.logical_not(fresh) & (core == section), stale[which].at[patch]),
                (jnp.logical_not(fresh) & (core != section), stale[2 + which].at[patch]),
            ]
            for condition, source in sources:
                @pl.when(condition)
                def _(source=source, place=place, sem=sem):
                    pltpu.make_async_copy(source, place, sem).start()
    copies = weight_copies(where_ref, size, shards, 0, buffer, sems)
    start_all(copies[0])
    for patch in range(patches):
        for which, target in enumerate((k_buf, v_buf)):
            place = target.at[:, pl.ds(patch * tokens, tokens)]
            pltpu.make_async_copy(stale[which].at[patch], place, kv_sems.at[2 * patch + which]).wait()
    keys = k_buf.shape[1]
    valid = lax.broadcasted_iota(jnp.int32, (1, keys), 1) < length_ref[0]
    factor = 1.0 / (math.sqrt(HD) * math.log(2.0))
    blocks = [None] * (wide // LANES)
    for head in range(heads):
        low, high = head * HD, head * HD + HD
        a = low // LANES * LANES
        b = min(-(-high // LANES) * LANES, width)
        lane = lax.broadcasted_iota(jnp.int32, (1, b - a), 1) + a
        inside = (lane >= low) & (lane < high)
        q = jnp.where(inside, query[:, a:b], jnp.zeros((), jnp.bfloat16))
        scores = jnp.dot(q, k_buf[a:b, :], preferred_element_type=jnp.float32)
        scores = jnp.where(valid, scores, -1e30)
        top = jnp.max(scores, axis=-1, keepdims=True)
        weights = jnp.exp2((scores - top) * factor)
        totals = jnp.sum(weights, axis=-1, keepdims=True)
        mixed = dot_nt(weights.astype(jnp.bfloat16), v_buf[a:b, :])
        mixed = jnp.where(inside, mixed / totals, 0.0)
        if (b - a) % LANES:
            mixed = jnp.concatenate([mixed, jnp.zeros((tokens, LANES - (b - a) % LANES), jnp.float32)], axis=1)
        for j in range(mixed.shape[1] // LANES):
            piece = mixed[:, j * LANES:(j + 1) * LANES]
            at = a // LANES + j
            blocks[at] = piece if blocks[at] is None else blocks[at] + piece
    attended = jnp.concatenate(blocks, axis=1).astype(jnp.bfloat16)
    wait_all(copies[0])
    out_ref[...] = dot_nt(attended, buffer[...]).astype(jnp.bfloat16)


def mlp_body(size, n_parts, where_ref, x_ref, own_ref, other_ref, mod_ref, *refs):
    ups, downs, refs = refs[:n_parts], refs[n_parts:2 * n_parts], refs[2 * n_parts:]
    x1_ref, out_ref, up_buf, up_sems, down_buf, down_sems = refs
    groups = [
        copies
        for pair in zip(weight_copies(where_ref, size, ups, 0, up_buf, up_sems),
                        weight_copies(where_ref, size, downs, 0, down_buf, down_sems))
        for copies in pair
    ]
    start_all(groups[0])
    start_all(groups[1])
    summed = own_ref[...].astype(jnp.float32) + other_ref[...].astype(jnp.float32)
    x1 = x_ref[...].astype(jnp.float32) + mod_ref[2:3, :] * summed
    x1_ref[...] = x1
    h = modulated(x1, mod_ref, 3, 4)
    step = up_buf.shape[1] // up_sems.shape[1]
    total = None
    for tile in range(up_sems.shape[1]):
        columns = slice(tile * step, (tile + 1) * step)
        for which in range(2):
            at = 2 * tile + which
            wait_all(groups[at])
            if at + 2 < len(groups):
                start_all(groups[at + 2])
            if which == 0:
                hidden = jnp.dot(h, up_buf[:, columns], preferred_element_type=jnp.float32)
                g = jax.nn.gelu(hidden, approximate=True).astype(jnp.bfloat16)
            else:
                part = dot_nt(g, down_buf[:, columns])
                total = part if total is None else total + part
    out_ref[...] = total.astype(jnp.bfloat16)


IN_SMEM = pl.BlockSpec(memory_space=pltpu.SMEM)
IN_VMEM = pl.BlockSpec(memory_space=pltpu.VMEM)
IN_HBM = pl.BlockSpec(memory_space=pl.ANY)


def call(body, name, args, specs, outs, scratch, microseconds):
    return pl.pallas_call(
        body,
        name=name,
        out_shape=outs,
        in_specs=specs,
        out_specs=[IN_VMEM] * len(outs),
        scratch_shapes=scratch,
        compiler_params=pltpu.CompilerParams(vmem_limit_bytes=VMEM_LIMIT),
        cost_estimate=pl.CostEstimate(flops=int(microseconds * 1e9), bytes_accessed=1 << 14, transcendentals=0),
    )(*args)


def shape_of(*dims, dtype=jnp.bfloat16):
    return jax.ShapeDtypeStruct(dims, dtype)


def partners(bit):
    return [(i, i ^ (1 << bit)) for i in range(lax.axis_size("row"))]


def all_steps(timesteps):
    n = lax.axis_size("row")
    if n & (n - 1):
        return lax.all_gather(timesteps, "row", axis=0, tiled=True)
    mine = jnp.arange(n) == lax.axis_index("row")
    steps = jnp.where(mine, timesteps, 0)
    for bit in range(n.bit_length() - 1):
        steps = steps + lax.ppermute(steps, "row", partners(bit))
    return steps


def row_sums(part):
    n = lax.axis_size("row")
    if n & (n - 1):
        return [lax.psum_scatter(part, "row", scatter_dimension=0, tiled=True)[0]]
    out = []
    for bit in reversed(range(n.bit_length() - 1)):
        half = part.shape[0] // 2
        high = (lax.axis_index("row") >> bit) & 1
        kept = jnp.where(high == 1, part[half:], part[:half])
        away = jnp.where(high == 1, part[:half], part[half:])
        part = kept + lax.ppermute(away, "row", partners(bit))
        out.append(part)
    return out[:-1] + [part[0]]


def modulation_parts(steps, ada_local):
    rows = ada_local.shape[0]
    cond = jax.nn.silu(sinusoid(steps, rows * lax.axis_size("row"))).astype(jnp.bfloat16)
    cond = lax.dynamic_slice_in_dim(cond, lax.axis_index("row") * rows, rows, 1)
    return jnp.einsum("rd,dkc->rkc", cond, ada_local, preferred_element_type=jnp.float32)


def both_modulations(summed):
    col, core = lax.axis_index("col"), lax.axis_index("section")
    other = lax.ppermute(summed, "col", SWAP)
    mine = jnp.where(col == 0, jnp.concatenate([summed, other], 1), jnp.concatenate([other, summed], 1))
    other = lax.ppermute(mine, "section", SWAP)
    return [jnp.where(core == s, mine, other) for s in range(2)]


def local(
    latents,
    timesteps,
    lengths,
    patch_order,
    ada_weight,
    qkv_weight,
    out_weight,
    up_weight,
    down_weight,
    stale_keys,
    stale_values,
):
    core = lax.axis_index("section")
    col = lax.axis_index("col")
    patches, shared_tokens, depth = latents.shape[1:]
    tokens = shared_tokens * 2
    per_core = patches // 2
    width = qkv_weight.shape[3]
    hidden = up_weight.shape[2]
    rows = qkv_weight.shape[1]
    wide = -(-width // LANES) * LANES
    ring = Ring(rows)
    size = ring.size
    n_parts = len(ring.counts)
    where = jnp.stack([core, lax.axis_index("row"), col]).astype(jnp.int32)

    def shards_of(piece, other):
        first = jnp.where(core == 0, piece, other)
        return first, lambda *gates: jnp.where(core == 1, after(piece, *gates), other)

    first_piece = jnp.concatenate([out_weight[0].T, qkv_weight[0].reshape(rows, 3 * width)], axis=1)
    steps = all_steps(timesteps)
    first_piece = after(first_piece, steps)
    shard, later = shards_of(first_piece, lax.ppermute(first_piece, "section", SWAP))
    pieces = [[shard, later]]

    first_patch = core * per_core
    own_half = lax.dynamic_slice_in_dim(latents[0], first_patch, per_core, 0)
    own_chunks = [own_half[i] for i in range(per_core)]
    with jax.named_scope("swap_latents"):
        other_chunks = [lax.ppermute(chunk, "col", SWAP) for chunk in own_chunks]

    class Travel:
        def __init__(self, name, shard, each=False):
            self.name, self.held, self.each = name, shard, each
            self.own, self.came, self.swapped = shard, [], []

        def swap(self, part):
            with jax.named_scope(f"{self.name}_cores{len(self.swapped) + 1}"):
                self.swapped.append(lax.ppermute(part, "section", SWAP))

        def go(self, *gates):
            if gates:
                self.held = after(self.held, *gates)
            for _ in range(ring.hops // 4):
                with jax.named_scope(f"{self.name}_hop{len(self.came) + 1}"):
                    self.held = ring.hop(len(self.came) + 1, self.held)
                self.came.append(self.held)
                if self.each and len(self.came) == ring.hops - 1:
                    for part in self.came:
                        self.swap(after(part, self.held))
            return self.held

        def laid(self, *gates):
            for i in range(len(self.swapped), ring.hops):
                last = i == ring.hops - 1
                self.swap(after(self.came[i], self.held, *(gates if last else ())))
            pairs = [part for pair in zip(self.came, self.swapped) for part in pair]
            return ring.lay([self.own] + pairs)

    first = Travel("attn0", pieces[0][0], each=True)
    hop1 = first.go()
    sums = row_sums(modulation_parts(steps, ada_weight[0]))
    pieces[0][1] = pieces[0][1](hop1)
    for piece in (up_weight[0], down_weight[0].T):
        piece = after(piece, hop1)
        shard, later = shards_of(piece, lax.ppermute(piece, "section", SWAP))
        pieces.append([shard, later(hop1)])
    stale = [jnp.swapaxes(cache, 1, 2) for cache in (stale_keys[0, 0], stale_values[0, 0])]
    stale += [lax.ppermute(after(cache, hop1), "section", SWAP) for cache in stale]
    first.go(other_chunks[0], sums[0])
    hop3 = first.go(other_chunks[1], sums[len(sums) // 2], pieces[1][0], pieces[2][0])
    hop4 = first.go(sums[-1], *stale[2:])
    mods = both_modulations(sums[-1])
    second, third = Travel("up0", pieces[1][0]), Travel("down0", pieces[2][0])
    second.go(hop3)
    third.go(hop4)

    weight_specs = [IN_HBM] * n_parts

    def weight_buffers(columns, tiles):
        return [pltpu.VMEM((rows * size, columns), jnp.bfloat16), pltpu.SemaphoreType.DMA((n_parts, tiles))]

    def project(s, chunks, args, shards):
        start = width // LANES * LANES
        outs = [shape_of(chunks, tokens, width)] + [shape_of(width, tokens)] * (2 * chunks)
        outs += [shape_of(tokens, depth)] * chunks
        return call(
            functools.partial(qkv_body, size, n_parts, width, chunks, s == 0), "qkv",
            [where] + args + shards, [IN_SMEM] + [IN_VMEM] * len(args) + weight_specs, outs,
            weight_buffers(4 * width - start, 1), 7)

    def attend(s, i, query, fresh_own, fresh_other, shards):
        return call(
            functools.partial(attend_body, size, n_parts, s, i, per_core), "attend",
            [where, patch_order, lengths, query] + fresh_own + fresh_other + stale + shards,
            [IN_SMEM] * 3 + [IN_VMEM] + [IN_HBM] * (4 * per_core + 4) + weight_specs,
            [shape_of(tokens, depth)],
            [pltpu.VMEM((width, patches * tokens), jnp.bfloat16)] * 2 + weight_buffers(wide, 1)
            + [pltpu.SemaphoreType.DMA((2 * patches,))], 8)[0]

    def mlp(x, own, other, mod, up_shards, down_shards):
        return call(
            functools.partial(mlp_body, size, n_parts), "mlp",
            [where, x, own, other, mod] + up_shards + down_shards,
            [IN_SMEM] + [IN_VMEM] * 4 + weight_specs * 2,
            [shape_of(tokens, depth, dtype=jnp.float32), shape_of(tokens, depth)],
            weight_buffers(hidden, 3) * 2, 9)

    def swap_col(x):
        return lax.ppermute(x, "col", SWAP)

    def swap_core(x):
        return lax.ppermute(x, "section", SWAP)

    def col_half(x):
        return lax.dynamic_slice_in_dim(x, col * shared_tokens, shared_tokens, 0)

    shards = first.laid()
    queries, *rest = project(0, per_core, own_chunks + other_chunks + [mods[0]], shards)
    fresh, x_chunks = rest[:2 * per_core], rest[2 * per_core:]
    fresh_other = [swap_core(x) for x in fresh]
    att, att_other = [None] * 2, [None] * 2
    second.go(queries)
    third.go(queries)
    att[0] = attend(0, 0, queries, fresh, fresh_other, shards)
    with jax.named_scope("swap_att"):
        att_other[0] = swap_col(att[0])
    second.go(att[0])
    att[1] = attend(0, 1, queries, fresh, fresh_other, shards)
    with jax.named_scope("swap_att"):
        att_other[1] = swap_col(att[1])
    third.go(att[0])
    second.go(att[1])
    third.go(att[1])
    first = Travel("attn1", pieces[0][1])
    first.go(second.came[1])
    first.go(att[1])
    up_shards, down_shards = second.laid(), third.laid(att[1], att_other[0])
    second, third = Travel("up1", pieces[1][1]), Travel("down1", pieces[2][1])
    second.go(att[1])
    third.go(att[1])
    x1, down, down_other = [None] * 2, [None] * 2, [None] * 2
    x1[0], down[0] = mlp(x_chunks[0], att[0], att_other[0], mods[0], up_shards, down_shards)
    with jax.named_scope("swap_down"):
        down_other[0] = swap_col(down[0])
    first.go(down[0], att_other[1])
    second.go(down[0])
    x1[1], down[1] = mlp(x_chunks[1], att[1], att_other[1], mods[0], up_shards, down_shards)
    with jax.named_scope("swap_down"):
        down_other[1] = swap_col(down[1])
    first.go(down[1], second.came[0], third.came[0])
    third.go(down[1])
    second.go(down[1])

    shards = first.laid(down[1], down_other[0])
    results = [None] * 2
    results[0] = project(1, 1, [x1[0], down[0], down_other[0], mods[0], mods[1]], shards)
    third.go(results[0][0])
    results[1] = project(1, 1, [x1[1], down[1], down_other[1], mods[0], mods[1]], shards)
    second.go(results[1][0])
    fresh = [x for result in results for x in result[1:3]]
    fresh_other = [swap_core(x if i else after(x, down_other[1])) for i, x in enumerate(fresh)]
    x_chunks = [result[3] for result in results]
    att[0] = attend(1, 0, results[0][0], fresh, fresh_other, shards)
    with jax.named_scope("swap_att"):
        att_other[0] = swap_col(att[0])
    third.go(att[0])
    att[1] = attend(1, 1, results[1][0], fresh, fresh_other, shards)
    with jax.named_scope("swap_att"):
        att_other[1] = swap_col(att[1])
    up_shards, down_shards = second.laid(), third.laid(att[1], att_other[0])
    chosen, before = [], None
    for i in range(2):
        x1, part = mlp(x_chunks[i], att[i], att_other[i], mods[1], up_shards, down_shards)
        away = lax.dynamic_slice_in_dim(part, (1 - col) * shared_tokens, shared_tokens, 0)
        with jax.named_scope("swap_last"):
            before = other = swap_col(away if before is None else after(away, before))
        summed = col_half(part).astype(jnp.float32) + other.astype(jnp.float32)
        late = (col_half(x1) + mods[1][5][None, :] * summed).astype(jnp.bfloat16)
        early = col_half(x_chunks[i])
        came = swap_core(jnp.where(core == 0, late, early))
        chosen.append((jnp.where(core == 0, early, late), came))
    kept = jnp.stack([pair[0] for pair in chosen])
    came = jnp.stack([pair[1] for pair in chosen])
    result = jnp.where(core == 0, jnp.concatenate([kept, came]), jnp.concatenate([came, kept]))
    return result[None, None]


def solution(mesh):
    return jax.shard_map(
        local,
        mesh=mesh,
        in_specs=(
            P("row", None, "col", None),
            P("row"),
            P("row"),
            P(),
            P("section", "row", None, "col"),
            P("section", "row", None, "col"),
            P("section", "col", "row"),
            P("section", "row", "col"),
            P("section", "col", "row"),
            P("section", "row", None, None, "col"),
            P("section", "row", None, None, "col"),
        ),
        out_specs=P("section", "row", None, "col", None),
        check_vma=False,
    )
```

```python
import functools
import math

import jax
import jax.numpy as jnp
from jax import lax
from jax.experimental import pallas as pl
from jax.experimental.pallas import tpu as pltpu
from jax.sharding import PartitionSpec as P

HD = 72
LANES = 128
SUBLANES = 16
SWAP = [(0, 1), (1, 0)]
VMEM_LIMIT = 62 * 1024 * 1024
COST = 1e9
GATES = {'attn0.2': 'l0 s0', 'attn0.3': 'l1 s1 u w', 'attn0.4': 's2 st', 'up0.1': 'attn0.3', 'down0.1': 'attn0.4', 'up0.2': 'q', 'down0.2': 'q', 'up0.3': 'a0', 'down0.3': 'a0', 'up0.4': 'a1', 'down0.4': 'a1', 'down0.z': 'a1 ao0', 'attn1.1': 'up0.2', 'attn1.2': 'a1', 'up1.1': 'a1', 'down1.1': 'd0', 'attn1.3': 'd0', 'up1.2': 'd0', 'attn1.4': 'd1 up1.1 down1.1', 'down1.2': 'd1', 'up1.3': 'd1', 'attn1.z': 'd1 do0', 'down1.3': 'r0', 'up1.4': 'r1', 'kv': 'do1', 'down1.4': 'b0', 'down1.z': 'b1 bo0', 'd1': 'attn1.1'}


def sinusoid(step_ids, width):
    half_width = width // 2
    frequency = jnp.exp(-math.log(10000.0) * jnp.arange(half_width, dtype=jnp.float32) / half_width)
    angles = step_ids.astype(jnp.float32)[:, None] * frequency[None, :]
    return jnp.concatenate([jnp.cos(angles), jnp.sin(angles)], axis=1)


def layer_norm(inputs):
    center = jnp.mean(inputs, axis=-1, keepdims=True)
    spread = jnp.mean(jnp.square(inputs - center), axis=-1, keepdims=True)
    return (inputs - center) * lax.rsqrt(spread + 1e-06)


def dot_nt(left, right):
    return lax.dot_general(left, right, (((1,), (1,)), ((), ())), preferred_element_type=jnp.float32)


def after(value, *others):
    return lax.optimization_barrier((value,) + others)[0]


def place_of(row, size):
    half = lax.div(row, 2)
    return jnp.where(lax.rem(row, 2) == 0, half, size - 1 - half)


def row_at(place, size):
    place = lax.rem(place + size, size)
    return jnp.where(place < size // 2, 2 * place, 2 * (size - 1 - place) + 1)


def half_rows(rows):
    half = (rows + 1) // 2
    if rows % SUBLANES == 0:
        half = -(-half // SUBLANES) * SUBLANES
    return half


def spots(core, row, size, rows):
    half = half_rows(rows)
    rest = rows - half
    here = place_of(row, size)
    back = jnp.where(core == 0, 1, -1)
    out = [(rows, 0, row * rows)]
    for hop in range(1, size // 2 + 1):
        near = row_at(here - hop * back, size) * rows
        far = row_at(here + hop * back, size) * rows
        if hop < size // 2:
            out += [(rows, 0, near), (rows, 0, far)]
        else:
            out += [
                (half, 0, near + jnp.where(core == 0, 0, rest)),
                (rest, jnp.where(core == 0, half - rest, 0), far + jnp.where(core == 0, half, 0)),
            ]
    return out


class Ring:
    def __init__(self, rows):
        self.core = lax.axis_index("section")
        self.size = lax.axis_size("row")
        self.rows = rows
        n = self.size
        order = list(range(0, n, 2)) + list(range(n - 1, 0, -2))
        self.pairs = [(order[i], order[(i + 1) % n]) for i in range(n)]
        self.pairs += [(n + order[(i + 1) % n], n + order[i]) for i in range(n)]
        self.hops = n // 2
        self.direct = rows % SUBLANES == 0
        if self.direct:
            self.counts = [spot[0] for spot in spots(0, 0, n, rows)]
        else:
            self.counts = [rows * n]

    def hop(self, number, held):
        if number == self.hops:
            half = half_rows(self.rows)
            held = jnp.where(self.core == 0, held[:half], held[self.rows - half:])
        return lax.ppermute(held, ("section", "row"), self.pairs)

    def lay(self, parts):
        if self.direct:
            return parts
        total = self.rows * self.size
        whole = jnp.zeros((total, parts[0].shape[1]), parts[0].dtype)
        for part, spot in zip(parts, spots(self.core, lax.axis_index("row"), self.size, self.rows)):
            block = lax.dynamic_slice_in_dim(part, spot[1], spot[0], 0)
            whole = lax.dynamic_update_slice_in_dim(whole, block, spot[2], 0)
        return [whole]


def weight_copies(where_ref, size, refs, first_column, buffer, sems):
    tiles = sems.shape[1]
    total, wide = buffer.shape
    step = wide // tiles
    rows = total // size
    if len(refs) == 1:
        places = [(total, 0, 0)]
    else:
        places = spots(where_ref[0], where_ref[1], size, rows)
    out = []
    for tile in range(tiles):
        copies = []
        for i, (ref, (count, first, place)) in enumerate(zip(refs, places)):
            if not isinstance(first, int):
                first = pl.multiple_of(first, SUBLANES)
            if not isinstance(place, int):
                place = pl.multiple_of(place, SUBLANES)
            copies.append(pltpu.make_async_copy(
                ref.at[pl.ds(first, count), pl.ds(first_column + tile * step, step)],
                buffer.at[pl.ds(place, count), pl.ds(tile * step, step)], sems.at[i, tile]))
        out.append(copies)
    return out


def start_all(copies):
    for copy in copies:
        copy.start()


def wait_all(copies):
    for copy in copies:
        copy.wait()


def modulated(x, mod_ref, shift, scale):
    return (layer_norm(x) * (1.0 + mod_ref[scale:scale + 1, :]) + mod_ref[shift:shift + 1, :]).astype(jnp.bfloat16)


def qkv_body(size, n_parts, width, chunks, first_layer, where_ref, *refs):
    if first_layer:
        own_refs, other_refs, mod_ref = refs[:chunks], refs[chunks:2 * chunks], refs[2 * chunks]
        refs = refs[2 * chunks + 1:]
    else:
        x1_ref, own_ref, other_ref, last_ref, mod_ref = refs[:5]
        refs = refs[5:]
    shards, refs = refs[:n_parts], refs[n_parts:]
    q_ref, kv_refs = refs[0], refs[1:1 + 2 * chunks]
    x_refs = refs[1 + 2 * chunks:-2]
    buffer, sems = refs[-2:]
    start = width // LANES * LANES
    copies = weight_copies(where_ref, size, shards, start, buffer, sems)
    for group in copies:
        start_all(group)
    if first_layer:
        first_half = where_ref[2] == 0
        halves = []
        for own, other in zip(own_refs, other_refs):
            own, other = own[...].astype(jnp.float32), other[...].astype(jnp.float32)
            halves += [jnp.where(first_half, own, other), jnp.where(first_half, other, own)]
        x = jnp.concatenate(halves, axis=0)
        tokens = x.shape[0] // chunks
        for i in range(chunks):
            x_refs[i][...] = x[i * tokens:(i + 1) * tokens].astype(jnp.bfloat16)
    else:
        summed = own_ref[...].astype(jnp.float32) + other_ref[...].astype(jnp.float32)
        x = (x1_ref[...] + last_ref[5:6, :] * summed).astype(jnp.bfloat16)
        x_refs[0][...] = x
        x = x.astype(jnp.float32)
    h = modulated(x, mod_ref, 0, 1)
    outs = []
    step = buffer.shape[1] // len(copies)
    for tile, waits in enumerate(copies):
        wait_all(waits)
        weight = buffer[:, tile * step:(tile + 1) * step]
        outs.append(jnp.dot(h, weight, preferred_element_type=jnp.float32).astype(jnp.bfloat16))
    out = jnp.concatenate(outs, axis=1)
    skip = width - start
    tokens = x.shape[0] // chunks
    for i in range(chunks):
        part = out[i * tokens:(i + 1) * tokens]
        q_ref[i] = part[:, skip:skip + width]
        for which in range(2):
            low = skip + (1 + which) * width
            kv_refs[2 * i + which][...] = part[:, low:low + width].T


def attend_body(size, n_parts, section, chunk, per_core, where_ref, order_ref, length_ref, q_ref, *refs):
    own, other, stale = refs[:2 * per_core], refs[2 * per_core:4 * per_core], refs[4 * per_core:4 * per_core + 4]
    refs = refs[4 * per_core + 4:]
    shards, refs = refs[:n_parts], refs[n_parts:]
    out_ref, k_buf, v_buf, buffer, sems, kv_sems = refs
    query = q_ref[0 if q_ref.shape[0] == 1 else chunk]
    tokens, width = query.shape
    heads = width // HD
    core = where_ref[0]
    wide = buffer.shape[1]
    patches = stale[0].shape[0]
    here = core * per_core + chunk
    positions = [sum(jnp.where(order_ref[j] == p, j, 0) for j in range(patches)) for p in range(patches)]
    position = sum(jnp.where(here == p, positions[p], 0) for p in range(patches))
    for patch in range(patches):
        fresh = positions[patch] <= position
        mine = core == patch // per_core
        slot = patch % per_core
        for which, target in enumerate((k_buf, v_buf)):
            place = target.at[:, pl.ds(patch * tokens, tokens)]
            sem = kv_sems.at[2 * patch + which]
            sources = [
                (fresh & mine, own[2 * slot + which]),
                (fresh & jnp.logical_not(mine), other[2 * slot + which]),
                (jnp.logical_not(fresh) & (core == section), stale[which].at[patch]),
                (jnp.logical_not(fresh) & (core != section), stale[2 + which].at[patch]),
            ]
            for condition, source in sources:
                @pl.when(condition)
                def _(source=source, place=place, sem=sem):
                    pltpu.make_async_copy(source, place, sem).start()
    copies = weight_copies(where_ref, size, shards, 0, buffer, sems)
    start_all(copies[0])
    for patch in range(patches):
        for which, target in enumerate((k_buf, v_buf)):
            place = target.at[:, pl.ds(patch * tokens, tokens)]
            pltpu.make_async_copy(stale[which].at[patch], place, kv_sems.at[2 * patch + which]).wait()
    keys = k_buf.shape[1]
    valid = lax.broadcasted_iota(jnp.int32, (1, keys), 1) < length_ref[0]
    factor = 1.0 / (math.sqrt(HD) * math.log(2.0))
    blocks = [None] * (wide // LANES)
    for head in range(heads):
        low, high = head * HD, head * HD + HD
        a = low // LANES * LANES
        b = min(-(-high // LANES) * LANES, width)
        lane = lax.broadcasted_iota(jnp.int32, (1, b - a), 1) + a
        inside = (lane >= low) & (lane < high)
        q = jnp.where(inside, query[:, a:b], jnp.zeros((), jnp.bfloat16))
        scores = jnp.dot(q, k_buf[a:b, :], preferred_element_type=jnp.float32)
        scores = jnp.where(valid, scores, -1e30)
        top = jnp.max(scores, axis=-1, keepdims=True)
        weights = jnp.exp2((scores - top) * factor)
        totals = jnp.sum(weights, axis=-1, keepdims=True)
        mixed = dot_nt(weights.astype(jnp.bfloat16), v_buf[a:b, :])
        mixed = jnp.where(inside, mixed / totals, 0.0)
        if (b - a) % LANES:
            mixed = jnp.concatenate([mixed, jnp.zeros((tokens, LANES - (b - a) % LANES), jnp.float32)], axis=1)
        for j in range(mixed.shape[1] // LANES):
            piece = mixed[:, j * LANES:(j + 1) * LANES]
            at = a // LANES + j
            blocks[at] = piece if blocks[at] is None else blocks[at] + piece
    attended = jnp.concatenate(blocks, axis=1).astype(jnp.bfloat16)
    wait_all(copies[0])
    out_ref[...] = dot_nt(attended, buffer[...]).astype(jnp.bfloat16)


def mlp_body(size, n_parts, where_ref, x_ref, own_ref, other_ref, mod_ref, *refs):
    ups, downs, refs = refs[:n_parts], refs[n_parts:2 * n_parts], refs[2 * n_parts:]
    x1_ref, out_ref, up_buf, up_sems, down_buf, down_sems = refs
    groups = [
        copies
        for pair in zip(weight_copies(where_ref, size, ups, 0, up_buf, up_sems),
                        weight_copies(where_ref, size, downs, 0, down_buf, down_sems))
        for copies in pair
    ]
    for group in groups[:3]:
        start_all(group)
    summed = own_ref[...].astype(jnp.float32) + other_ref[...].astype(jnp.float32)
    x1 = x_ref[...].astype(jnp.float32) + mod_ref[2:3, :] * summed
    x1_ref[...] = x1
    h = modulated(x1, mod_ref, 3, 4)
    step = up_buf.shape[1] // up_sems.shape[1]
    total = None
    for tile in range(up_sems.shape[1]):
        columns = slice(tile * step, (tile + 1) * step)
        for which in range(2):
            at = 2 * tile + which
            wait_all(groups[at])
            if at + 3 < len(groups):
                start_all(groups[at + 3])
            if which == 0:
                hidden = jnp.dot(h, up_buf[:, columns], preferred_element_type=jnp.float32)
                g = jax.nn.gelu(hidden, approximate=True).astype(jnp.bfloat16)
            else:
                part = dot_nt(g, down_buf[:, columns])
                total = part if total is None else total + part
    out_ref[...] = total.astype(jnp.bfloat16)


IN_SMEM = pl.BlockSpec(memory_space=pltpu.SMEM)
IN_VMEM = pl.BlockSpec(memory_space=pltpu.VMEM)
IN_HBM = pl.BlockSpec(memory_space=pl.ANY)


def call(body, name, args, specs, outs, scratch, microseconds):
    return pl.pallas_call(
        body,
        name=name,
        out_shape=outs,
        in_specs=specs,
        out_specs=[IN_VMEM] * len(outs),
        scratch_shapes=scratch,
        compiler_params=pltpu.CompilerParams(vmem_limit_bytes=VMEM_LIMIT),
        cost_estimate=pl.CostEstimate(flops=int(microseconds * COST), bytes_accessed=1 << 14, transcendentals=0),
    )(*args)


def shape_of(*dims, dtype=jnp.bfloat16):
    return jax.ShapeDtypeStruct(dims, dtype)


def partners(bit):
    return [(i, i ^ (1 << bit)) for i in range(lax.axis_size("row"))]


def all_steps(timesteps):
    n = lax.axis_size("row")
    if n & (n - 1):
        return lax.all_gather(timesteps, "row", axis=0, tiled=True)
    mine = jnp.arange(n) == lax.axis_index("row")
    steps = jnp.where(mine, timesteps, 0)
    for bit in range(n.bit_length() - 1):
        steps = steps + lax.ppermute(steps, "row", partners(bit))
    return steps


def row_sums(part):
    n = lax.axis_size("row")
    if n & (n - 1):
        return [lax.psum_scatter(part, "row", scatter_dimension=0, tiled=True)[0]]
    out = []
    for bit in reversed(range(n.bit_length() - 1)):
        half = part.shape[0] // 2
        high = (lax.axis_index("row") >> bit) & 1
        kept = jnp.where(high == 1, part[half:], part[:half])
        away = jnp.where(high == 1, part[:half], part[half:])
        part = kept + lax.ppermute(away, "row", partners(bit))
        out.append(part)
    return out[:-1] + [part[0]]


def modulation_parts(steps, ada_local):
    rows = ada_local.shape[0]
    cond = jax.nn.silu(sinusoid(steps, rows * lax.axis_size("row"))).astype(jnp.bfloat16)
    cond = lax.dynamic_slice_in_dim(cond, lax.axis_index("row") * rows, rows, 1)
    return jnp.einsum("rd,dkc->rkc", cond, ada_local, preferred_element_type=jnp.float32)


def both_modulations(summed):
    col, core = lax.axis_index("col"), lax.axis_index("section")
    other = lax.ppermute(summed, "col", SWAP)
    mine = jnp.where(col == 0, jnp.concatenate([summed, other], 1), jnp.concatenate([other, summed], 1))
    other = lax.ppermute(mine, "section", SWAP)
    return [jnp.where(core == s, mine, other) for s in range(2)]


def local(
    latents,
    timesteps,
    lengths,
    patch_order,
    ada_weight,
    qkv_weight,
    out_weight,
    up_weight,
    down_weight,
    stale_keys,
    stale_values,
):
    core = lax.axis_index("section")
    col = lax.axis_index("col")
    patches, shared_tokens, depth = latents.shape[1:]
    tokens = shared_tokens * 2
    per_core = patches // 2
    width = qkv_weight.shape[3]
    hidden = up_weight.shape[2]
    rows = qkv_weight.shape[1]
    wide = -(-width // LANES) * LANES
    ring = Ring(rows)
    size = ring.size
    n_parts = len(ring.counts)
    where = jnp.stack([core, lax.axis_index("row"), col]).astype(jnp.int32)

    first_patch = core * per_core
    own_half = lax.dynamic_slice_in_dim(latents[0], first_patch, per_core, 0)
    own_chunks = [own_half[i] for i in range(per_core)]

    values = {}

    def step(name):
        if name not in values:
            values[name] = steps_of[name]()
        return values[name]

    def gated(value, name):
        names = GATES.get(name, "").split()
        return after(value, *[step(other) for other in names]) if names else value

    def hops(piece, shard):
        def go(number):
            def run():
                held = shard() if number == 1 else step(f"{piece}.{number - 1}")
                held = gated(held, f"{piece}.{number}")
                for i in range(ring.hops // 4):
                    at = (number - 1) * (ring.hops // 4) + i + 1
                    with jax.named_scope(f"{piece}_hop{at}"):
                        held = ring.hop(at, held)
                    came.append(held)
                return held
            return run

        came = []
        for number in range(1, 5):
            steps_of[f"{piece}.{number}"] = go(number)

        def parts():
            last = step(f"{piece}.4")
            most = step(f"{piece}.3") if piece == "attn0" else last
            swapped = []
            for i, part in enumerate(came):
                with jax.named_scope(f"{piece}_cores{i + 1}"):
                    if i < ring.hops - 1:
                        part = gated(after(part, most), f"{piece}.w")
                    else:
                        part = gated(part, f"{piece}.z")
                    swapped.append(lax.ppermute(part, "section", SWAP))
            return ring.lay([shard()] + [part for pair in zip(came, swapped) for part in pair])

        steps_of[piece] = parts

    def swap_col(x):
        return lax.ppermute(x, "col", SWAP)

    def swap_core(x):
        return lax.ppermute(x, "section", SWAP)

    def sections_shards(name, piece):
        steps_of[name + "_swapped"] = lambda: swap_core(piece())
        for s in range(2):
            steps_of[f"{name}{s}_shard"] = lambda s=s: jnp.where(
                core == s, after(piece(), *([step(f"{name}0.1")] if s else [])), step(name + "_swapped"))

    steps_of = {"steps": lambda: all_steps(timesteps)}
    first_piece = jnp.concatenate([out_weight[0].T, qkv_weight[0].reshape(rows, 3 * width)], axis=1)
    sections_shards("attn", lambda: after(first_piece, step("steps")))
    sections_shards("up", lambda: after(up_weight[0], step("attn0.1")))
    sections_shards("down", lambda: after(down_weight[0].T, step("attn0.1")))
    for name in ("attn", "up", "down"):
        for s in range(2):
            hops(f"{name}{s}", lambda name=name, s=s: step(f"{name}{s}_shard"))
    steps_of["u"] = lambda: step("up0_shard")
    steps_of["w"] = lambda: step("down0_shard")

    def swapped_latents(i):
        with jax.named_scope("swap_latents"):
            return swap_col(gated(own_chunks[i], f"l{i}"))

    for i in range(per_core):
        steps_of[f"l{i}"] = functools.partial(swapped_latents, i)
    steps_of["sums"] = lambda: row_sums(modulation_parts(step("steps"), ada_weight[0]))
    for i in range(3):
        steps_of[f"s{i}"] = lambda i=i: step("sums")[i * (len(step("sums")) - 1) // 2]
    steps_of["mods"] = lambda: both_modulations(step("s2"))
    caches = [jnp.swapaxes(cache, 1, 2) for cache in (stale_keys[0, 0], stale_values[0, 0])]
    steps_of["stale"] = lambda: caches + [swap_core(gated(after(cache, step("attn0.1")), "stale")) for cache in caches]
    steps_of["st"] = lambda: step("stale")[-1]

    weight_specs = [IN_HBM] * n_parts

    def weight_buffers(columns, tiles):
        return [pltpu.VMEM((rows * size, columns), jnp.bfloat16), pltpu.SemaphoreType.DMA((n_parts, tiles))]

    def project(s, chunks, args, shards):
        start = width // LANES * LANES
        outs = [shape_of(chunks, tokens, width)] + [shape_of(width, tokens)] * (2 * chunks)
        outs += [shape_of(tokens, depth)] * chunks
        return call(
            functools.partial(qkv_body, size, n_parts, width, chunks, s == 0), "qkv",
            [where] + args + shards, [IN_SMEM] + [IN_VMEM] * len(args) + weight_specs, outs,
            weight_buffers(4 * width - start, 1), 7)

    def attend(s, i, query, fresh_own, fresh_other, shards):
        return call(
            functools.partial(attend_body, size, n_parts, s, i, per_core), "attend",
            [where, patch_order, lengths, query] + fresh_own + fresh_other + step("stale") + shards,
            [IN_SMEM] * 3 + [IN_VMEM] + [IN_HBM] * (4 * per_core + 4) + weight_specs,
            [shape_of(tokens, depth)],
            [pltpu.VMEM((width, patches * tokens), jnp.bfloat16)] * 2 + weight_buffers(wide, 1)
            + [pltpu.SemaphoreType.DMA((2 * patches,))], 8)[0]

    def mlp(x, own, other, mod, up_shards, down_shards):
        return call(
            functools.partial(mlp_body, size, n_parts), "mlp",
            [where, x, own, other, mod] + up_shards + down_shards,
            [IN_SMEM] + [IN_VMEM] * 4 + weight_specs * 2,
            [shape_of(tokens, depth, dtype=jnp.float32), shape_of(tokens, depth)],
            weight_buffers(hidden, 3) * 2, 9)

    def col_half(x):
        return lax.dynamic_slice_in_dim(x, col * shared_tokens, shared_tokens, 0)

    def project0():
        args = own_chunks + [step(f"l{i}") for i in range(per_core)] + [step("mods")[0]]
        return project(0, per_core, [gated(args[0], "q")] + args[1:], step("attn0"))

    def project1(i):
        args = [step(f"d{i}x"), step(f"d{i}"), step(f"do{i}"), step("mods")[0], step("mods")[1]]
        return project(1, 1, [gated(args[0], f"r{i}")] + args[1:], step("attn1"))

    def neighbours(name, source):
        def run():
            with jax.named_scope("swap_" + source):
                return swap_col(gated(step(source), name))
        return run

    def attend_with(s, i):
        query = step("q") if s == 0 else step(f"r{i}")
        fresh, other = step(f"kv{s}"), step(f"kvo{s}")
        return attend(s, i, gated(query, "ab"[s] + str(i)), fresh, other, step(f"attn{s}"))

    def mlp_of(s, i):
        name = "ab"[s]
        x = gated(step(f"x{s}")[i], "de"[s] + str(i))
        return mlp(x, step(f"{name}{i}"), step(f"{name}o{i}"), step("mods")[s], step(f"up{s}"), step(f"down{s}"))

    steps_of["project0"] = project0
    steps_of["q"] = lambda: step("project0")[0]
    steps_of["kv0"] = lambda: list(step("project0")[1:1 + 2 * per_core])
    steps_of["x0"] = lambda: list(step("project0")[1 + 2 * per_core:])
    steps_of["kvo0"] = lambda: [swap_core(x) for x in step("kv0")]
    steps_of["kv1"] = lambda: [x for i in range(per_core) for x in step(f"project1{i}")[1:3]]
    steps_of["x1"] = lambda: [step(f"project1{i}")[3] for i in range(per_core)]
    steps_of["kvo1"] = lambda: [swap_core(x if i else gated(x, "kv")) for i, x in enumerate(step("kv1"))]
    for i in range(per_core):
        steps_of[f"project1{i}"] = functools.partial(project1, i)
        steps_of[f"r{i}"] = lambda i=i: step(f"project1{i}")[0]
        steps_of[f"mlp0{i}"] = functools.partial(mlp_of, 0, i)
        steps_of[f"mlp1{i}"] = functools.partial(mlp_of, 1, i)
        steps_of[f"d{i}x"] = lambda i=i: step(f"mlp0{i}")[0]
        steps_of[f"d{i}"] = lambda i=i: step(f"mlp0{i}")[1]
        steps_of[f"do{i}"] = neighbours(f"do{i}", f"d{i}")
        for s in range(2):
            steps_of["ab"[s] + str(i)] = functools.partial(attend_with, s, i)
            steps_of["ab"[s] + f"o{i}"] = neighbours("ab"[s] + f"o{i}", "ab"[s] + str(i))

    for name in ("attn0", "q", "a0", "a1", "up0", "down0", "d0", "d1", "attn1", "r0", "r1", "b0", "b1", "up1", "down1"):
        step(name)
    chosen, before = [], None
    for i in range(per_core):
        x1, part = step(f"mlp1{i}")
        away = lax.dynamic_slice_in_dim(part, (1 - col) * shared_tokens, shared_tokens, 0)
        with jax.named_scope("swap_last"):
            before = other = swap_col(away if before is None else after(away, before))
        summed = col_half(part).astype(jnp.float32) + other.astype(jnp.float32)
        late = (col_half(x1) + step("mods")[1][5][None, :] * summed).astype(jnp.bfloat16)
        early = col_half(step("x1")[i])
        came = swap_core(jnp.where(core == 0, late, early))
        chosen.append((jnp.where(core == 0, early, late), came))
    kept = jnp.stack([pair[0] for pair in chosen])
    came = jnp.stack([pair[1] for pair in chosen])
    result = jnp.where(core == 0, jnp.concatenate([kept, came]), jnp.concatenate([came, kept]))
    return result[None, None]


def solution(mesh):
    return jax.shard_map(
        local,
        mesh=mesh,
        in_specs=(
            P("row", None, "col", None),
            P("row"),
            P("row"),
            P(),
            P("section", "row", None, "col"),
            P("section", "row", None, "col"),
            P("section", "col", "row"),
            P("section", "row", "col"),
            P("section", "col", "row"),
            P("section", "row", None, None, "col"),
            P("section", "row", None, None, "col"),
        ),
        out_specs=P("section", "row", None, "col", None),
        check_vma=False,
    )
```

```python
import functools
import math

import jax
import jax.numpy as jnp
from jax import lax
from jax.experimental import pallas as pl
from jax.experimental.pallas import tpu as pltpu
from jax.sharding import PartitionSpec as P

HD = 72
LANES = 128
SUBLANES = 16
SWAP = [(0, 1), (1, 0)]
VMEM_LIMIT = 62 * 1024 * 1024


def sinusoid(step_ids, width):
    half_width = width // 2
    frequency = jnp.exp(-math.log(10000.0) * jnp.arange(half_width, dtype=jnp.float32) / half_width)
    angles = step_ids.astype(jnp.float32)[:, None] * frequency[None, :]
    return jnp.concatenate([jnp.cos(angles), jnp.sin(angles)], axis=1)


def layer_norm(inputs):
    center = jnp.mean(inputs, axis=-1, keepdims=True)
    spread = jnp.mean(jnp.square(inputs - center), axis=-1, keepdims=True)
    return (inputs - center) * lax.rsqrt(spread + 1e-06)


def dot_nt(left, right):
    return lax.dot_general(left, right, (((1,), (1,)), ((), ())), preferred_element_type=jnp.float32)


def after(value, *others):
    return lax.optimization_barrier((value,) + others)[0]


def place_of(row, size):
    half = lax.div(row, 2)
    return jnp.where(lax.rem(row, 2) == 0, half, size - 1 - half)


def row_at(place, size):
    place = lax.rem(place + size, size)
    return jnp.where(place < size // 2, 2 * place, 2 * (size - 1 - place) + 1)


def half_rows(rows):
    half = (rows + 1) // 2
    if rows % SUBLANES == 0:
        half = -(-half // SUBLANES) * SUBLANES
    return half


def spots(core, row, size, rows):
    half = half_rows(rows)
    rest = rows - half
    here = place_of(row, size)
    back = jnp.where(core == 0, 1, -1)
    out = [(rows, 0, row * rows)]
    for hop in range(1, size // 2 + 1):
        near = row_at(here - hop * back, size) * rows
        far = row_at(here + hop * back, size) * rows
        if hop < size // 2:
            out += [(rows, 0, near), (rows, 0, far)]
        else:
            out += [
                (half, 0, near + jnp.where(core == 0, 0, rest)),
                (rest, jnp.where(core == 0, half - rest, 0), far + jnp.where(core == 0, half, 0)),
            ]
    return out


class Ring:
    def __init__(self, rows):
        self.core = lax.axis_index("section")
        self.size = lax.axis_size("row")
        self.rows = rows
        n = self.size
        order = list(range(0, n, 2)) + list(range(n - 1, 0, -2))
        self.pairs = [(order[i], order[(i + 1) % n]) for i in range(n)]
        self.pairs += [(n + order[(i + 1) % n], n + order[i]) for i in range(n)]
        self.hops = n // 2
        self.direct = rows % SUBLANES == 0
        if self.direct:
            self.counts = [spot[0] for spot in spots(0, 0, n, rows)]
        else:
            self.counts = [rows * n]

    def hop(self, number, held):
        if number == self.hops:
            half = half_rows(self.rows)
            held = jnp.where(self.core == 0, held[:half], held[self.rows - half:])
        return lax.ppermute(held, ("section", "row"), self.pairs)

    def lay(self, parts):
        if self.direct:
            return parts
        total = self.rows * self.size
        whole = jnp.zeros((total, parts[0].shape[1]), parts[0].dtype)
        for part, spot in zip(parts, spots(self.core, lax.axis_index("row"), self.size, self.rows)):
            block = lax.dynamic_slice_in_dim(part, spot[1], spot[0], 0)
            whole = lax.dynamic_update_slice_in_dim(whole, block, spot[2], 0)
        return [whole]


def weight_copies(where_ref, size, refs, first_column, buffer, sems):
    tiles = sems.shape[1]
    total, wide = buffer.shape
    step = wide // tiles
    rows = total // size
    if len(refs) == 1:
        places = [(total, 0, 0)]
    else:
        places = spots(where_ref[0], where_ref[1], size, rows)
    out = []
    for tile in range(tiles):
        copies = []
        for i, (ref, (count, first, place)) in enumerate(zip(refs, places)):
            if not isinstance(first, int):
                first = pl.multiple_of(first, SUBLANES)
            if not isinstance(place, int):
                place = pl.multiple_of(place, SUBLANES)
            copies.append(pltpu.make_async_copy(
                ref.at[pl.ds(first, count), pl.ds(first_column + tile * step, step)],
                buffer.at[pl.ds(place, count), pl.ds(tile * step, step)], sems.at[i, tile]))
        out.append(copies)
    return out


def start_all(copies):
    for copy in copies:
        copy.start()


def wait_all(copies):
    for copy in copies:
        copy.wait()


def modulated(x, mod_ref, shift, scale):
    return (layer_norm(x) * (1.0 + mod_ref[scale:scale + 1, :]) + mod_ref[shift:shift + 1, :]).astype(jnp.bfloat16)


def qkv_body(size, n_parts, width, chunks, first_layer, where_ref, *refs):
    if first_layer:
        own_refs, other_refs, mod_ref = refs[:chunks], refs[chunks:2 * chunks], refs[2 * chunks]
        refs = refs[2 * chunks + 1:]
    else:
        x1_ref, own_ref, other_ref, last_ref, mod_ref = refs[:5]
        refs = refs[5:]
    shards, refs = refs[:n_parts], refs[n_parts:]
    q_ref, kv_refs = refs[0], refs[1:1 + 2 * chunks]
    x_refs = refs[1 + 2 * chunks:-2]
    buffer, sems = refs[-2:]
    start = width // LANES * LANES
    copies = weight_copies(where_ref, size, shards, start, buffer, sems)
    for group in copies:
        start_all(group)
    if first_layer:
        first_half = where_ref[2] == 0
        halves = []
        for own, other in zip(own_refs, other_refs):
            own, other = own[...].astype(jnp.float32), other[...].astype(jnp.float32)
            halves += [jnp.where(first_half, own, other), jnp.where(first_half, other, own)]
        x = jnp.concatenate(halves, axis=0)
        tokens = x.shape[0] // chunks
        for i in range(chunks):
            x_refs[i][...] = x[i * tokens:(i + 1) * tokens].astype(jnp.bfloat16)
    else:
        summed = own_ref[...].astype(jnp.float32) + other_ref[...].astype(jnp.float32)
        x = (x1_ref[...] + last_ref[5:6, :] * summed).astype(jnp.bfloat16)
        x_refs[0][...] = x
        x = x.astype(jnp.float32)
    h = modulated(x, mod_ref, 0, 1)
    outs = []
    step = buffer.shape[1] // len(copies)
    for tile, waits in enumerate(copies):
        wait_all(waits)
        weight = buffer[:, tile * step:(tile + 1) * step]
        outs.append(jnp.dot(h, weight, preferred_element_type=jnp.float32).astype(jnp.bfloat16))
    out = jnp.concatenate(outs, axis=1)
    skip = width - start
    tokens = x.shape[0] // chunks
    for i in range(chunks):
        part = out[i * tokens:(i + 1) * tokens]
        q_ref[i] = part[:, skip:skip + width]
        for which in range(2):
            low = skip + (1 + which) * width
            kv_refs[2 * i + which][...] = part[:, low:low + width].T


def attend_body(size, n_parts, section, chunk, per_core, where_ref, order_ref, length_ref, q_ref, *refs):
    own, other, stale = refs[:2 * per_core], refs[2 * per_core:4 * per_core], refs[4 * per_core:4 * per_core + 4]
    refs = refs[4 * per_core + 4:]
    shards, refs = refs[:n_parts], refs[n_parts:]
    out_ref, k_buf, v_buf, buffer, sems, kv_sems = refs
    query = q_ref[0 if q_ref.shape[0] == 1 else chunk]
    tokens, width = query.shape
    heads = width // HD
    core = where_ref[0]
    wide = buffer.shape[1]
    patches = stale[0].shape[0]
    here = core * per_core + chunk
    positions = [sum(jnp.where(order_ref[j] == p, j, 0) for j in range(patches)) for p in range(patches)]
    position = sum(jnp.where(here == p, positions[p], 0) for p in range(patches))
    for patch in range(patches):
        fresh = positions[patch] <= position
        mine = core == patch // per_core
        slot = patch % per_core
        for which, target in enumerate((k_buf, v_buf)):
            place = target.at[:, pl.ds(patch * tokens, tokens)]
            sem = kv_sems.at[2 * patch + which]
            sources = [
                (fresh & mine, own[2 * slot + which]),
                (fresh & jnp.logical_not(mine), other[2 * slot + which]),
                (jnp.logical_not(fresh) & (core == section), stale[which].at[patch]),
                (jnp.logical_not(fresh) & (core != section), stale[2 + which].at[patch]),
            ]
            for condition, source in sources:
                @pl.when(condition)
                def _(source=source, place=place, sem=sem):
                    pltpu.make_async_copy(source, place, sem).start()
    copies = weight_copies(where_ref, size, shards, 0, buffer, sems)
    start_all(copies[0])
    for patch in range(patches):
        for which, target in enumerate((k_buf, v_buf)):
            place = target.at[:, pl.ds(patch * tokens, tokens)]
            pltpu.make_async_copy(stale[which].at[patch], place, kv_sems.at[2 * patch + which]).wait()
    keys = k_buf.shape[1]
    valid = lax.broadcasted_iota(jnp.int32, (1, keys), 1) < length_ref[0]
    factor = 1.0 / (math.sqrt(HD) * math.log(2.0))
    blocks = [None] * (wide // LANES)
    for head in range(heads):
        low, high = head * HD, head * HD + HD
        a = low // LANES * LANES
        b = min(-(-high // LANES) * LANES, width)
        lane = lax.broadcasted_iota(jnp.int32, (1, b - a), 1) + a
        inside = (lane >= low) & (lane < high)
        q = jnp.where(inside, query[:, a:b], jnp.zeros((), jnp.bfloat16))
        scores = jnp.dot(q, k_buf[a:b, :], preferred_element_type=jnp.float32)
        scores = jnp.where(valid, scores, -1e30)
        top = jnp.max(scores, axis=-1, keepdims=True)
        weights = jnp.exp2((scores - top) * factor)
        totals = jnp.sum(weights, axis=-1, keepdims=True)
        mixed = dot_nt(weights.astype(jnp.bfloat16), v_buf[a:b, :])
        mixed = jnp.where(inside, mixed / totals, 0.0)
        if (b - a) % LANES:
            mixed = jnp.concatenate([mixed, jnp.zeros((tokens, LANES - (b - a) % LANES), jnp.float32)], axis=1)
        for j in range(mixed.shape[1] // LANES):
            piece = mixed[:, j * LANES:(j + 1) * LANES]
            at = a // LANES + j
            blocks[at] = piece if blocks[at] is None else blocks[at] + piece
    attended = jnp.concatenate(blocks, axis=1).astype(jnp.bfloat16)
    wait_all(copies[0])
    out_ref[...] = dot_nt(attended, buffer[...]).astype(jnp.bfloat16)


def mlp_body(size, n_parts, where_ref, x_ref, own_ref, other_ref, mod_ref, *refs):
    ups, downs, refs = refs[:n_parts], refs[n_parts:2 * n_parts], refs[2 * n_parts:]
    x1_ref, out_ref, up_buf, up_sems, down_buf, down_sems = refs
    groups = [
        copies
        for pair in zip(weight_copies(where_ref, size, ups, 0, up_buf, up_sems),
                        weight_copies(where_ref, size, downs, 0, down_buf, down_sems))
        for copies in pair
    ]
    for group in groups[:3]:
        start_all(group)
    summed = own_ref[...].astype(jnp.float32) + other_ref[...].astype(jnp.float32)
    x1 = x_ref[...].astype(jnp.float32) + mod_ref[2:3, :] * summed
    x1_ref[...] = x1
    h = modulated(x1, mod_ref, 3, 4)
    step = up_buf.shape[1] // up_sems.shape[1]
    total = None
    for tile in range(up_sems.shape[1]):
        columns = slice(tile * step, (tile + 1) * step)
        for which in range(2):
            at = 2 * tile + which
            wait_all(groups[at])
            if at + 3 < len(groups):
                start_all(groups[at + 3])
            if which == 0:
                hidden = jnp.dot(h, up_buf[:, columns], preferred_element_type=jnp.float32)
                g = jax.nn.gelu(hidden, approximate=True).astype(jnp.bfloat16)
            else:
                part = dot_nt(g, down_buf[:, columns])
                total = part if total is None else total + part
    out_ref[...] = total.astype(jnp.bfloat16)


IN_SMEM = pl.BlockSpec(memory_space=pltpu.SMEM)
IN_VMEM = pl.BlockSpec(memory_space=pltpu.VMEM)
IN_HBM = pl.BlockSpec(memory_space=pl.ANY)


def call(body, name, args, specs, outs, scratch, microseconds):
    return pl.pallas_call(
        body,
        name=name,
        out_shape=outs,
        in_specs=specs,
        out_specs=[IN_VMEM] * len(outs),
        scratch_shapes=scratch,
        compiler_params=pltpu.CompilerParams(vmem_limit_bytes=VMEM_LIMIT),
        cost_estimate=pl.CostEstimate(flops=int(microseconds * 1e9), bytes_accessed=1 << 14, transcendentals=0),
    )(*args)


def shape_of(*dims, dtype=jnp.bfloat16):
    return jax.ShapeDtypeStruct(dims, dtype)


def partners(bit):
    return [(i, i ^ (1 << bit)) for i in range(lax.axis_size("row"))]


def all_steps(timesteps):
    n = lax.axis_size("row")
    if n & (n - 1):
        return lax.all_gather(timesteps, "row", axis=0, tiled=True)
    mine = jnp.arange(n) == lax.axis_index("row")
    steps = jnp.where(mine, timesteps, 0)
    for bit in range(n.bit_length() - 1):
        steps = steps + lax.ppermute(steps, "row", partners(bit))
    return steps


def row_sums(part):
    n = lax.axis_size("row")
    if n & (n - 1):
        return [lax.psum_scatter(part, "row", scatter_dimension=0, tiled=True)[0]]
    out = []
    for bit in reversed(range(n.bit_length() - 1)):
        half = part.shape[0] // 2
        high = (lax.axis_index("row") >> bit) & 1
        kept = jnp.where(high == 1, part[half:], part[:half])
        away = jnp.where(high == 1, part[:half], part[half:])
        part = kept + lax.ppermute(away, "row", partners(bit))
        out.append(part)
    return out[:-1] + [part[0]]


def modulation_parts(steps, ada_local):
    rows = ada_local.shape[0]
    cond = jax.nn.silu(sinusoid(steps, rows * lax.axis_size("row"))).astype(jnp.bfloat16)
    cond = lax.dynamic_slice_in_dim(cond, lax.axis_index("row") * rows, rows, 1)
    return jnp.einsum("rd,dkc->rkc", cond, ada_local, preferred_element_type=jnp.float32)


def both_modulations(summed):
    col, core = lax.axis_index("col"), lax.axis_index("section")
    other = lax.ppermute(summed, "col", SWAP)
    mine = jnp.where(col == 0, jnp.concatenate([summed, other], 1), jnp.concatenate([other, summed], 1))
    other = lax.ppermute(mine, "section", SWAP)
    return [jnp.where(core == s, mine, other) for s in range(2)]


def local(
    latents,
    timesteps,
    lengths,
    patch_order,
    ada_weight,
    qkv_weight,
    out_weight,
    up_weight,
    down_weight,
    stale_keys,
    stale_values,
):
    core = lax.axis_index("section")
    col = lax.axis_index("col")
    patches, shared_tokens, depth = latents.shape[1:]
    tokens = shared_tokens * 2
    per_core = patches // 2
    width = qkv_weight.shape[3]
    hidden = up_weight.shape[2]
    rows = qkv_weight.shape[1]
    wide = -(-width // LANES) * LANES
    ring = Ring(rows)
    size = ring.size
    n_parts = len(ring.counts)
    where = jnp.stack([core, lax.axis_index("row"), col]).astype(jnp.int32)

    def shards_of(piece, other):
        first = jnp.where(core == 0, piece, other)
        return first, lambda *gates: jnp.where(core == 1, after(piece, *gates), other)

    first_piece = jnp.concatenate([out_weight[0].T, qkv_weight[0].reshape(rows, 3 * width)], axis=1)
    steps = all_steps(timesteps)
    first_piece = after(first_piece, steps)
    shard, later = shards_of(first_piece, lax.ppermute(first_piece, "section", SWAP))
    pieces = [[shard, later]]

    first_patch = core * per_core
    own_half = lax.dynamic_slice_in_dim(latents[0], first_patch, per_core, 0)
    own_chunks = [own_half[i] for i in range(per_core)]
    with jax.named_scope("swap_latents"):
        other_chunks = [lax.ppermute(chunk, "col", SWAP) for chunk in own_chunks]

    class Travel:
        def __init__(self, name, shard, each=False):
            self.name, self.held, self.each = name, shard, each
            self.own, self.came, self.swapped = shard, [], []

        def swap(self, part):
            with jax.named_scope(f"{self.name}_cores{len(self.swapped) + 1}"):
                self.swapped.append(lax.ppermute(part, "section", SWAP))

        def go(self, *gates):
            if gates:
                self.held = after(self.held, *gates)
            for _ in range(ring.hops // 4):
                with jax.named_scope(f"{self.name}_hop{len(self.came) + 1}"):
                    self.held = ring.hop(len(self.came) + 1, self.held)
                self.came.append(self.held)
                if self.each and len(self.came) == ring.hops - 1:
                    for part in self.came:
                        self.swap(after(part, self.held))
            return self.held

        def laid(self, *gates):
            for i in range(len(self.swapped), ring.hops):
                last = i == ring.hops - 1
                self.swap(after(self.came[i], self.held, *(gates if last else ())))
            pairs = [part for pair in zip(self.came, self.swapped) for part in pair]
            return ring.lay([self.own] + pairs)

    first = Travel("attn0", pieces[0][0], each=True)
    hop1 = first.go()
    sums = row_sums(modulation_parts(steps, ada_weight[0]))
    pieces[0][1] = pieces[0][1](hop1)
    for piece in (up_weight[0], down_weight[0].T):
        piece = after(piece, hop1)
        shard, later = shards_of(piece, lax.ppermute(piece, "section", SWAP))
        pieces.append([shard, later(hop1)])
    stale = [jnp.swapaxes(cache, 1, 2) for cache in (stale_keys[0, 0], stale_values[0, 0])]
    stale += [lax.ppermute(after(cache, hop1), "section", SWAP) for cache in stale]
    first.go(other_chunks[0], sums[0])
    hop3 = first.go(other_chunks[1], sums[len(sums) // 2], pieces[1][0], pieces[2][0])
    hop4 = first.go(sums[-1], *stale[2:])
    mods = both_modulations(sums[-1])
    second, third = Travel("up0", pieces[1][0]), Travel("down0", pieces[2][0])
    second.go(hop3)
    third.go(hop4)

    weight_specs = [IN_HBM] * n_parts

    def weight_buffers(columns, tiles):
        return [pltpu.VMEM((rows * size, columns), jnp.bfloat16), pltpu.SemaphoreType.DMA((n_parts, tiles))]

    def project(s, chunks, args, shards):
        start = width // LANES * LANES
        outs = [shape_of(chunks, tokens, width)] + [shape_of(width, tokens)] * (2 * chunks)
        outs += [shape_of(tokens, depth)] * chunks
        return call(
            functools.partial(qkv_body, size, n_parts, width, chunks, s == 0), "qkv",
            [where] + args + shards, [IN_SMEM] + [IN_VMEM] * len(args) + weight_specs, outs,
            weight_buffers(4 * width - start, 1), 7)

    def attend(s, i, query, fresh_own, fresh_other, shards):
        return call(
            functools.partial(attend_body, size, n_parts, s, i, per_core), "attend",
            [where, patch_order, lengths, query] + fresh_own + fresh_other + stale + shards,
            [IN_SMEM] * 3 + [IN_VMEM] + [IN_HBM] * (4 * per_core + 4) + weight_specs,
            [shape_of(tokens, depth)],
            [pltpu.VMEM((width, patches * tokens), jnp.bfloat16)] * 2 + weight_buffers(wide, 1)
            + [pltpu.SemaphoreType.DMA((2 * patches,))], 8)[0]

    def mlp(x, own, other, mod, up_shards, down_shards):
        return call(
            functools.partial(mlp_body, size, n_parts), "mlp",
            [where, x, own, other, mod] + up_shards + down_shards,
            [IN_SMEM] + [IN_VMEM] * 4 + weight_specs * 2,
            [shape_of(tokens, depth, dtype=jnp.float32), shape_of(tokens, depth)],
            weight_buffers(hidden, 3) * 2, 9)

    def swap_col(x):
        return lax.ppermute(x, "col", SWAP)

    def swap_core(x):
        return lax.ppermute(x, "section", SWAP)

    def col_half(x):
        return lax.dynamic_slice_in_dim(x, col * shared_tokens, shared_tokens, 0)

    shards = first.laid()
    queries, *rest = project(0, per_core, own_chunks + other_chunks + [mods[0]], shards)
    fresh, x_chunks = rest[:2 * per_core], rest[2 * per_core:]
    fresh_other = [swap_core(x) for x in fresh]
    att, att_other = [None] * 2, [None] * 2
    second.go(queries)
    third.go(queries)
    att[0] = attend(0, 0, queries, fresh, fresh_other, shards)
    with jax.named_scope("swap_att"):
        att_other[0] = swap_col(att[0])
    second.go(att[0])
    att[1] = attend(0, 1, queries, fresh, fresh_other, shards)
    with jax.named_scope("swap_att"):
        att_other[1] = swap_col(att[1])
    third.go(att[0])
    second.go(att[1])
    third.go(att[1])
    first = Travel("attn1", pieces[0][1])
    first.go(second.came[1])
    first.go(att[1])
    up_shards, down_shards = second.laid(), third.laid(att[1], att_other[0])
    second, third = Travel("up1", pieces[1][1]), Travel("down1", pieces[2][1])
    second.go(att[1])
    x1, down, down_other = [None] * 2, [None] * 2, [None] * 2
    x1[0], down[0] = mlp(x_chunks[0], att[0], att_other[0], mods[0], up_shards, down_shards)
    with jax.named_scope("swap_down"):
        down_other[0] = swap_col(down[0])
    first.go(down[0])
    third.go(down[0])
    second.go(down[0])
    x1[1], down[1] = mlp(after(x_chunks[1], first.came[0]), att[1], att_other[1], mods[0], up_shards, down_shards)
    with jax.named_scope("swap_down"):
        down_other[1] = swap_col(down[1])
    first.go(down[1], second.came[0], third.came[0])
    third.go(down[1])
    second.go(down[1])

    shards = first.laid(down[1], down_other[0])
    results = [None] * 2
    results[0] = project(1, 1, [x1[0], down[0], down_other[0], mods[0], mods[1]], shards)
    third.go(results[0][0])
    results[1] = project(1, 1, [x1[1], down[1], down_other[1], mods[0], mods[1]], shards)
    second.go(results[1][0])
    fresh = [x for result in results for x in result[1:3]]
    fresh_other = [swap_core(x if i else after(x, down_other[1])) for i, x in enumerate(fresh)]
    x_chunks = [result[3] for result in results]
    att[0] = attend(1, 0, results[0][0], fresh, fresh_other, shards)
    with jax.named_scope("swap_att"):
        att_other[0] = swap_col(att[0])
    third.go(att[0])
    att[1] = attend(1, 1, results[1][0], fresh, fresh_other, shards)
    with jax.named_scope("swap_att"):
        att_other[1] = swap_col(att[1])
    up_shards, down_shards = second.laid(), third.laid(att[1], att_other[0])
    chosen, before = [], None
    for i in range(2):
        x1, part = mlp(x_chunks[i], att[i], att_other[i], mods[1], up_shards, down_shards)
        away = lax.dynamic_slice_in_dim(part, (1 - col) * shared_tokens, shared_tokens, 0)
        with jax.named_scope("swap_last"):
            before = other = swap_col(away if before is None else after(away, before))
        summed = col_half(part).astype(jnp.float32) + other.astype(jnp.float32)
        late = (col_half(x1) + mods[1][5][None, :] * summed).astype(jnp.bfloat16)
        early = col_half(x_chunks[i])
        came = swap_core(jnp.where(core == 0, late, early))
        chosen.append((jnp.where(core == 0, early, late), came))
    kept = jnp.stack([pair[0] for pair in chosen])
    came = jnp.stack([pair[1] for pair in chosen])
    result = jnp.where(core == 0, jnp.concatenate([kept, came]), jnp.concatenate([came, kept]))
    return result[None, None]


def solution(mesh):
    return jax.shard_map(
        local,
        mesh=mesh,
        in_specs=(
            P("row", None, "col", None),
            P("row"),
            P("row"),
            P(),
            P("section", "row", None, "col"),
            P("section", "row", None, "col"),
            P("section", "col", "row"),
            P("section", "row", "col"),
            P("section", "col", "row"),
            P("section", "row", None, None, "col"),
            P("section", "row", None, None, "col"),
        ),
        out_specs=P("section", "row", None, "col", None),
        check_vma=False,
    )
```
